256 devices in a mesh: dp: 8 (over x, y_hi), tm: 2 (over y_lo), space: 16 (over z, core).
Axes of the slice: x: 4, y: 4 (y_hi: 2, y_lo: 2; y = y_hi * 2 + y_lo), z: 8, core: 2. Of those that a mesh axis runs over, the one named last changes fastest.
Arguments:
- latents: bfloat16 [256, 4, 256, 512], P(('dp', 'tm', 'space')), parts along dimension 0, may hold values from -36 to 36, as said below
- norm_gain: float32 [512], replicated, may hold values from 0.1 to 1.9
- conv_weight: bfloat16 [3, 3, 3, 512, 256], replicated, may hold values from -0.0546875 to 0.0546875
- skip_weight: bfloat16 [512, 256], replicated, may hold values from -0.25 to 0.25
- cotangent: bfloat16 [256, 16, 4, 16, 256], P(('dp', 'tm'), 'space'), parts along dimension 0, may hold values from -6 to 6
Outputs:
- output: bfloat16 [256, 16, 4, 16, 256], P(('dp', 'tm'), 'space'), parts along dimension 0
- grad_input: bfloat16 [256, 16, 4, 16, 512], P(('dp', 'tm'), 'space'), parts along dimension 0
The draws below stay inside these ranges and needn't reach their ends.
There are 8 independent parts, one for each index of `dp`. The reference program is written for one: setup_inputs(seed, part) draws one part's arguments, and reference() takes and returns one part's arrays. A program takes and returns all parts, laid end to end along the dimension named above; an argument that names none is the same for every part. Nothing has to cross between parts.
Inputs may be any that keep to these rules, and one draw needn't show every extreme that they name: `latents`: each cell and each channel has its own scale.
All inputs are finite; a program needn't handle non-finite values.
Results may differ from the reference program's by a relative error of at most 0.002.
Values may be sent and summed in bfloat16 or wider, within the bound.
A program may use at most 192 MiB of HBM per device.

```python
import math
import jax
import jax.numpy as jnp
from jax import lax

C_IN = 512
C_OUT = 256
HEIGHT = 4
TW = 16
WIDTH = 256
FRAMES = 32
TILES = 16
N_SPACE = 16


def draw_latents(key, part):
    first, second, third = jax.random.split(key, 3)
    shape = (FRAMES, HEIGHT, WIDTH, C_IN)
    cell_scale = jnp.exp(jax.random.uniform(second, (FRAMES, HEIGHT, WIDTH, 1), jnp.float32, math.log(0.3), math.log(3.0)))
    chan_scale = jnp.exp(jax.random.uniform(third, (C_IN,), jnp.float32, math.log(0.3), math.log(3.0)))
    base = jnp.clip(jax.random.normal(first, shape, jnp.float32), -4.0, 4.0)
    return (base * cell_scale * chan_scale).astype(jnp.bfloat16)


def block_levels(stream_key, shape, cuts, low, top_value):
    gain, own = 1.0, jax.random.fold_in(stream_key, 6)
    for position, shards_of in cuts:
        steps = jnp.exp(jax.random.uniform(jax.random.fold_in(own, position), (shards_of,), jnp.float32, low / len(cuts), top_value / len(cuts)))
        gain = gain * jnp.repeat(steps, shape[position] // shards_of).reshape([-1 if axis == position else 1 for axis in range(len(shape))])
    return gain


def noise(own_key, extent, spread, bound, pieces=(), kind=jnp.bfloat16):
    loudness = block_levels(own_key, extent, pieces, -0.22, 0.18) if pieces else 1.0
    values = jax.random.normal(own_key, extent, jnp.float32) * spread * loudness
    return jnp.minimum(jnp.maximum(values, -bound), bound).astype(kind)


def setup_inputs(seed: int = 0, part: int = 0) -> dict:
    splits = jax.random.split(jax.random.key(seed), 6)
    part_keys = jax.random.split(jax.random.fold_in(splits[5], part), 6)
    return {
        "latents": draw_latents(jax.random.fold_in(jax.random.fold_in(splits[5], part), 71), part),
        "norm_gain": jnp.clip(1.0 + 0.18 * jax.random.normal(splits[1], (C_IN,), jnp.float32), 0.1, 1.9),
        "conv_weight": noise(splits[2], (3, 3, 3, C_IN, C_OUT), (27 * C_IN) ** -0.5, 0.0546875),
        "skip_weight": noise(splits[3], (C_IN, C_OUT), C_IN ** -0.5, 0.25),
        "cotangent": noise(part_keys[4], (FRAMES, TILES, HEIGHT, TW, C_OUT), 1.0, 6.0, ((0, 2), (1, 16))),
    }


epsilon = 1e-06

def activate(x_float, norm_gain):
    mean_sq = lax.optimization_barrier(jnp.mean(x_float * x_float, axis=-1, keepdims=True))
    inv_rms = lax.rsqrt(mean_sq + epsilon)
    unit_val = x_float * inv_rms
    return (inv_rms, unit_val, unit_val * norm_gain)

def silu_slope(normed):
    sigma_val = jax.nn.sigmoid(normed)
    return sigma_val * (1.0 + normed * (1.0 - sigma_val))

def to_tiles(whole, strips):
    frames, height, width, channels = whole.shape
    shaped = whole.reshape(frames, height, strips, width // strips, channels)
    return shaped.transpose(0, 2, 1, 3, 4)

def from_tiles(tiled):
    frames, count, height, tile_cols, channels = tiled.shape
    return tiled.transpose(0, 2, 1, 3, 4).reshape(frames, height, count * tile_cols, channels)

def reference(latents, norm_gain, conv_weight, skip_weight, cotangent):
    frames, height, width, in_chan = latents.shape
    out_chan = skip_weight.shape[1]
    x_float = latents.astype(jnp.float32)
    inv_rms, unit_val, normed = activate(x_float, norm_gain)
    hidden = jax.nn.silu(normed).astype(jnp.bfloat16)
    padded = jnp.pad(hidden, ((2, 0), (1, 1), (1, 1), (0, 0)))
    summed = jnp.dot(latents.reshape(-1, in_chan), skip_weight, preferred_element_type=jnp.float32)
    for t_tap in range(3):
        for h_tap in range(3):
            for w_tap in range(3):
                window = padded[t_tap:t_tap + frames, h_tap:h_tap + height, w_tap:w_tap + width]
                summed = summed + jnp.dot(window.reshape(-1, in_chan), conv_weight[t_tap, h_tap, w_tap], preferred_element_type=jnp.float32)
    output = summed.astype(jnp.bfloat16).reshape(frames, height, width, out_chan)
    grad_out = from_tiles(cotangent)
    grad_pad = jnp.pad(grad_out, ((0, 2), (1, 1), (1, 1), (0, 0)))
    grad_hidden = jnp.zeros((frames * height * width, in_chan), jnp.float32)
    for t_tap in range(3):
        for h_tap in range(3):
            for w_tap in range(3):
                window = grad_pad[2 - t_tap:2 - t_tap + frames, 2 - h_tap:2 - h_tap + height, 2 - w_tap:2 - w_tap + width]
                grad_hidden = grad_hidden + jnp.dot(window.reshape(-1, out_chan), conv_weight[t_tap, h_tap, w_tap].T, preferred_element_type=jnp.float32)
    grad_skip = jnp.dot(grad_out.reshape(-1, out_chan), skip_weight.T, preferred_element_type=jnp.float32)
    grad_unit = grad_hidden.reshape(frames, height, width, in_chan) * silu_slope(normed) * norm_gain
    grad_input = inv_rms * (grad_unit - unit_val * lax.optimization_barrier(jnp.mean(grad_unit * unit_val, axis=-1, keepdims=True)))
    grad_input = grad_input + grad_skip.reshape(frames, height, width, in_chan)
    return (to_tiles(output, N_SPACE), to_tiles(grad_input.astype(jnp.bfloat16), N_SPACE))
```

```python
import jax
import jax.numpy as jnp
from jax import lax
from jax.experimental import pallas as pl
from jax.experimental.pallas import tpu as pltpu
from jax.sharding import PartitionSpec as P

MESH = pl.DeviceIdType.MESH
F32 = jnp.float32
BF16 = jnp.bfloat16
EPS = 1e-06
STRIPS = 16
CHIPS = STRIPS // 2
ROWS = 4
COLS = 16
CIN = 512
COUT = 256
CELLS = STRIPS * ROWS * COLS
LINES = STRIPS * ROWS
PAD = 8
NT = (((1,), (1,)), ((), ()))


def activate(x, gain):
    inv = lax.rsqrt(jnp.mean(x * x, axis=-1, keepdims=True) + EPS)
    unit = x * inv
    normed = unit * gain
    sig = 1.0 / (1.0 + jnp.exp(-normed))
    return inv, unit, normed, sig


def mm(a, b):
    return jnp.dot(a, b, preferred_element_type=F32)


def kernel(
    lat, gain_hbm, w_hbm, sk_hbm, cot_hbm, out_hbm, gi_hbm,
    w, sk, gain, cot, arr, arrp, cotn, cedge, chalo, wide, grads, gh, gs,
    hid, pad, edge, halo, hrows, stage, acc, obuf, gbuf,
    local_sem, own_sem, a_send, a_recv, c_send, c_recv, n_send, n_recv,
    h_send, h_recv, p_send, p_recv, out_sem,
):
    me = lax.axis_index("space")
    tm = lax.axis_index("tm")
    chip = me // 2
    other = 1 - tm
    left, right = lax.rem(me + STRIPS - 1, STRIPS), lax.rem(me + 1, STRIPS)
    sides = ((0, right, COLS - 1), (1, left, 0))

    barrier = pltpu.get_barrier_semaphore()
    for k in range(1, STRIPS):
        pl.semaphore_signal(
            barrier, inc=1, device_id={"space": lax.rem(me + k, STRIPS)}, device_id_type=MESH
        )
    for s in (me, left, right):
        pl.semaphore_signal(
            barrier, inc=1, device_id={"space": s, "tm": other}, device_id_type=MESH
        )

    loads = [
        pltpu.make_async_copy(source, target, local_sem.at[i])
        for i, (source, target) in enumerate(
            ((cot_hbm, cot), (sk_hbm, sk), (gain_hbm, gain), (w_hbm, w))
        )
    ]
    for load in loads:
        load.start()
    own = pltpu.make_async_copy(
        lat.at[:, pl.ds(pl.multiple_of(me * COLS, COLS), COLS), :],
        arr.at[pl.ds(me * ROWS, ROWS)],
        own_sem,
    )
    own.start()

    loads[0].wait()
    wide[0:LINES, PAD : PAD + COLS] = cot[...].astype(F32)
    for slot, _, col in sides:
        cedge[slot] = wide[0:LINES, PAD + col, :].astype(BF16)

    pl.semaphore_wait(barrier, STRIPS - 1 + 3)

    started = []
    for slot, target, _ in sides:
        started.append(
            pltpu.make_async_remote_copy(
                src_ref=cedge.at[slot],
                dst_ref=chalo.at[slot, pl.ds(0, LINES)],
                send_sem=c_send.at[slot, 0],
                recv_sem=c_recv.at[slot, 0],
                device_id={"space": target},
                device_id_type=MESH,
            )
        )
        started.append(
            pltpu.make_async_remote_copy(
                src_ref=cedge.at[slot, pl.ds(0, 16)],
                dst_ref=chalo.at[slot, pl.ds(LINES, 16)],
                send_sem=c_send.at[slot, 1],
                recv_sem=c_recv.at[slot, 1],
                device_id={"space": target, "tm": other},
                device_id_type=MESH,
            )
        )
    started.append(
        pltpu.make_async_remote_copy(
            src_ref=cot.at[pl.ds(0, 2 * ROWS)],
            dst_ref=cotn,
            send_sem=n_send,
            recv_sem=n_recv,
            device_id={"tm": other},
            device_id_type=MESH,
        )
    )
    for copy in started:
        copy.start()

    def strip_copy(target, source, i):
        return pltpu.make_async_remote_copy(
            src_ref=lat.at[:, pl.ds(pl.multiple_of(target * COLS, COLS), COLS), :],
            dst_ref=arr.at[pl.ds(source * ROWS, ROWS)],
            send_sem=a_send.at[i],
            recv_sem=a_recv.at[source],
            device_id={"space": target},
            device_id_type=MESH,
        )

    def target_of(i):
        step = i // 2
        if i == 0:
            return chip * 2 + (1 - me % 2)
        step = (i + 1) // 2
        dist = (step + 1) // 2 * (1 if step % 2 else -1)
        return lax.rem(chip + dist + CHIPS, CHIPS) * 2 + lax.rem(me + i, 2)

    sends = [strip_copy(target_of(i), me, i) for i in range(STRIPS - 1)]
    for copy in sends:
        copy.start()

    hid[...] = jnp.zeros_like(hid)
    grads[...] = jnp.zeros_like(grads)
    pad[...] = jnp.zeros_like(pad)
    loads[1].wait()
    loads[2].wait()
    gs[...] = lax.dot_general(
        cot[...].reshape(CELLS, COUT), sk[...], NT, preferred_element_type=F32
    ).reshape(LINES, COLS, CIN)

    for copy in started:
        copy.wait_recv()
    first = jnp.where(tm == 0, 1.0, 0.0)
    second = 1.0 - first
    wide[LINES:, PAD : PAD + COLS] = cotn[...].astype(F32) * first
    has = (jnp.where(me > 0, 1.0, 0.0), jnp.where(me < STRIPS - 1, 1.0, 0.0))
    for slot, sublane in ((0, PAD - 1), (1, PAD + COLS)):
        wide[0:LINES, sublane, :] = chalo[slot, 0:LINES].astype(F32) * has[slot]
        after = chalo[slot, LINES : LINES + 16].astype(F32)[0:8]
        wide[LINES : LINES + 8, sublane, :] = after * (has[slot] * first)

    def spread(f, carry):
        lines = pl.ds(f * ROWS, ROWS)
        for tap in range(3):
            at = PAD + 1 - tap
            grads[f, 1 : 1 + ROWS, :, tap * COUT : (tap + 1) * COUT] = wide[
                lines, at : at + COLS
            ].astype(BF16)
        return carry

    lax.fori_loop(0, STRIPS + 2, spread, 0)

    loads[3].wait()
    gh[...] = jnp.zeros_like(gh)

    def backward(k, carry):
        t, h = k // 3, lax.rem(k, 3)
        part = jnp.zeros((CELLS, CIN), F32)
        for tap in range(3):
            window = grads[
                pl.ds(2 - t, STRIPS), pl.ds(2 - h, ROWS), :, tap * COUT : (tap + 1) * COUT
            ].reshape(CELLS, COUT)
            part = part + lax.dot_general(
                window, w[k, tap * CIN : (tap + 1) * CIN], NT, preferred_element_type=F32
            )
        gh[...] += part.reshape(LINES, COLS, CIN)
        return carry

    lax.fori_loop(0, 9, backward, 0)

    own.wait()

    def put_hidden(i, line, hidden):
        pad[pl.ds(2 * i, 2), PAD : PAD + COLS] = hidden.astype(F32).reshape(2, COLS, CIN)
        f, r = line // 6, lax.rem(line, 6)
        rows = pl.ds(r, 2)
        hid[f, rows, :, 0:CIN] = pad[pl.ds(2 * i, 2), PAD - 1 : PAD - 1 + COLS].astype(BF16)
        hid[f, rows, :, CIN : 2 * CIN] = hidden.reshape(2, COLS, CIN)
        hid[f, rows, :, 2 * CIN :] = pad[pl.ds(2 * i, 2), PAD + 1 : PAD + 1 + COLS].astype(BF16)

    def arrive(k, carry):
        step = (k + 1) // 2
        dist = jnp.where(lax.rem(k, 2) == 1, step, -step)
        c = lax.rem(chip + dist + CHIPS, CHIPS)
        for i in range(2):
            source = 2 * c + i

            @pl.when(source != me)
            def _():
                strip_copy(me, source, 0).wait_recv()

        def lines(i, carry):
            rows = pl.ds(c * 8 + 2 * i, 2)
            x = arr[rows].astype(F32).reshape(2 * COLS, CIN)
            inv, unit, normed, sig = activate(x, gain[...])
            put_hidden(i, (2 * c + 2 + i // 2) * 6 + 1 + lax.rem(i, 2) * 2, (normed * sig).astype(BF16))
            slope = sig * (1.0 + normed * (1.0 - sig))
            gu = gh[rows].reshape(2 * COLS, CIN) * slope * gain[...]
            gx = inv * (gu - unit * jnp.mean(gu * unit, axis=-1, keepdims=True))
            gx = gx + gs[rows].reshape(2 * COLS, CIN)
            gbuf[rows] = gx.astype(BF16).reshape(2, COLS, CIN)
            return carry

        lax.fori_loop(0, 4, lines, 0)
        for slot, target, col in sides:
            edge[slot, c] = pad[:, PAD + col, :]
            edge_copy(slot, target, c).start()
        rows = pl.ds(c * 8, 8)
        pltpu.make_async_copy(gbuf.at[rows], gi_hbm.at[rows], out_sem.at[1 + c]).start()
        return carry

    def edge_copy(slot, target, c):
        return pltpu.make_async_remote_copy(
            src_ref=edge.at[slot, c],
            dst_ref=halo.at[slot, pl.ds((c + 1) * 8, 8)],
            send_sem=h_send.at[slot, c],
            recv_sem=h_recv.at[slot, c],
            device_id={"space": target},
            device_id_type=MESH,
        )

    before = [
        pltpu.make_async_remote_copy(
            src_ref=arr.at[pl.ds(LINES - 8, 8)],
            dst_ref=arrp,
            send_sem=p_send.at[2],
            recv_sem=p_recv.at[2],
            device_id={"tm": other},
            device_id_type=MESH,
        )
    ]
    for slot, target, _ in sides:
        before.append(
            pltpu.make_async_remote_copy(
                src_ref=edge.at[slot, CHIPS - 1],
                dst_ref=halo.at[slot, pl.ds(0, 8)],
                send_sem=p_send.at[slot],
                recv_sem=p_recv.at[slot],
                device_id={"space": target, "tm": other},
                device_id_type=MESH,
            )
        )

    def forward(j, carry):
        lo = jnp.where(j == 0, 0, 2 * j + 1)
        hi = jnp.minimum(2 * j + 3, CHIPS)
        lax.fori_loop(lo, hi, arrive, 0)

        @pl.when(j == 3)
        def _():
            for copy in before:
                copy.start()

        c1 = lax.rem(chip - j + CHIPS, CHIPS)
        c2 = lax.rem(chip + j + 1, CHIPS)
        half = 2 * ROWS * COLS
        stage[0:half] = mm(arr[pl.ds(c1 * 8, 8)].reshape(half, CIN), sk[...])
        stage[half:] = mm(arr[pl.ds(c2 * 8, 8)].reshape(half, CIN), sk[...])

        def taps(t, carry):
            total = stage[...]
            for h in range(3):
                window = jnp.concatenate(
                    [hid[pl.ds(2 * c + t, 2), h : h + ROWS] for c in (c1, c2)], axis=0
                ).reshape(2 * half, 3 * CIN)
                total = total + mm(window, w[3 * t + h])
            stage[...] = total
            return carry

        lax.fori_loop(0, 3, taps, 0)
        acc[pl.ds(c1 * 8, 8)] = stage[0:half].reshape(8, COLS, COUT)
        acc[pl.ds(c2 * 8, 8)] = stage[half:].reshape(8, COLS, COUT)
        return carry

    lax.fori_loop(0, 4, forward, 0)

    before[0].wait_recv()

    def lines_before(i, carry):
        x = arrp[pl.ds(2 * i, 2)].astype(F32).reshape(2 * COLS, CIN)
        _, _, normed, sig = activate(x, gain[...])
        put_hidden(i, (i // 2) * 6 + 1 + lax.rem(i, 2) * 2, (normed * sig * second).astype(BF16))
        return carry

    lax.fori_loop(0, 4, lines_before, 0)
    frame = ROWS * COLS
    both = acc[0 : 2 * ROWS].reshape(2 * frame, COUT)
    one = jnp.zeros((frame, COUT), F32)
    for h in range(3):
        both = both + mm(hid[0:2, h : h + ROWS].reshape(2 * frame, 3 * CIN), w[h])
        one = one + mm(hid[1, h : h + ROWS].reshape(frame, 3 * CIN), w[3 + h])
    acc[0 : 2 * ROWS] = both.reshape(2 * ROWS, COLS, COUT)
    acc[0:ROWS] += one.reshape(ROWS, COLS, COUT)

    for slot, target, _ in sides:

        def wait_edges(c, carry):
            edge_copy(slot, target, c).wait_recv()
            return carry

        lax.fori_loop(0, CHIPS, wait_edges, 0)
        before[1 + slot].wait_recv()
    count = LINES + 8
    for slot, tap, col in ((0, 0, 0), (1, 2, COLS - 1)):
        row = lax.rem(lax.broadcasted_iota(jnp.int32, (count, CIN), 0), ROWS)
        line = lax.broadcasted_iota(jnp.int32, (count, CIN), 0)
        value = halo[slot] * (has[slot] * jnp.where(line < 8, second, 1.0))
        hrows[:, 0:CIN] = jnp.where(row == 0, 0.0, pltpu.roll(value, 1, 0))
        hrows[:, CIN : 2 * CIN] = value
        hrows[:, 2 * CIN :] = jnp.where(row == ROWS - 1, 0.0, pltpu.roll(value, count - 1, 0))
        total = jnp.zeros((LINES, COUT), F32)
        for t in range(3):
            window = hrows[t * ROWS : t * ROWS + LINES].astype(BF16)
            for h in range(3):
                total = total + mm(
                    window[:, h * CIN : (h + 1) * CIN],
                    w[3 * t + h, tap * CIN : (tap + 1) * CIN],
                )
        acc[:, col, :] = acc[:, col, :] + total

    obuf[...] = acc[...].astype(BF16)
    result = pltpu.make_async_copy(obuf, out_hbm, out_sem.at[0])
    result.start()

    for copy in sends + started + before:
        copy.wait_send()
    for slot, target, _ in sides:

        def wait_sent(c, carry):
            edge_copy(slot, target, c).wait_send()
            return carry

        lax.fori_loop(0, CHIPS, wait_sent, 0)

    def wait_out(c, carry):
        rows = pl.ds(c * 8, 8)
        pltpu.make_async_copy(gbuf.at[rows], gi_hbm.at[rows], out_sem.at[1 + c]).wait()
        return carry

    lax.fori_loop(0, CHIPS, wait_out, 0)
    result.wait()


def local(latents, norm_gain, conv_weight, skip_weight, cotangent):
    hbm = pl.BlockSpec(memory_space=pl.ANY)
    dma = pltpu.SemaphoreType.DMA
    out, grad_input = pl.pallas_call(
        kernel,
        out_shape=(
            jax.ShapeDtypeStruct((LINES, COLS, COUT), BF16),
            jax.ShapeDtypeStruct((LINES, COLS, CIN), BF16),
        ),
        in_specs=[hbm] * 5,
        out_specs=(hbm, hbm),
        scratch_shapes=[
            pltpu.VMEM((9, 3 * CIN, COUT), BF16),
            pltpu.VMEM((CIN, COUT), BF16),
            pltpu.VMEM((1, CIN), F32),
            pltpu.VMEM((LINES, COLS, COUT), BF16),
            pltpu.VMEM((LINES, COLS, CIN), BF16),
            pltpu.VMEM((8, COLS, CIN), BF16),
            pltpu.VMEM((8, COLS, COUT), BF16),
            pltpu.VMEM((2, LINES, COUT), BF16),
            pltpu.VMEM((2, LINES + 16, COUT), BF16),
            pltpu.VMEM((LINES + 8, 32, COUT), F32),
            pltpu.VMEM((STRIPS + 2, ROWS + 2, COLS, 3 * COUT), BF16),
            pltpu.VMEM((LINES, COLS, CIN), F32),
            pltpu.VMEM((LINES, COLS, CIN), F32),
            pltpu.VMEM((STRIPS + 2, ROWS + 2, COLS, 3 * CIN), BF16),
            pltpu.VMEM((8, 32, CIN), F32),
            pltpu.VMEM((2, CHIPS, 8, CIN), F32),
            pltpu.VMEM((2, LINES + 8, CIN), F32),
            pltpu.VMEM((LINES + 8, 3 * CIN), F32),
            pltpu.VMEM((4 * ROWS * COLS, COUT), F32),
            pltpu.VMEM((LINES, COLS, COUT), F32),
            pltpu.VMEM((LINES, COLS, COUT), BF16),
            pltpu.VMEM((LINES, COLS, CIN), BF16),
            dma((4,)),
            dma,
            dma((STRIPS - 1,)),
            dma((STRIPS,)),
            dma((2, 2)),
            dma((2, 2)),
            dma,
            dma,
            dma((2, CHIPS)),
            dma((2, CHIPS)),
            dma((3,)),
            dma((3,)),
            dma((1 + CHIPS,)),
        ],
        compiler_params=pltpu.CompilerParams(
            collective_id=0, has_side_effects=True, vmem_limit_bytes=56 * 2**20
        ),
        cost_estimate=pl.CostEstimate(
            flops=2 * CELLS * CIN * COUT * 56, bytes_accessed=11 * 2**20, transcendentals=CELLS * CIN
        ),
    )(
        latents.reshape(ROWS, STRIPS * COLS, CIN),
        norm_gain.reshape(1, CIN),
        conv_weight.reshape(9, 3 * CIN, COUT),
        skip_weight,
        cotangent.reshape(LINES, COLS, COUT),
    )
    return (
        out.reshape(STRIPS, 1, ROWS, COLS, COUT),
        grad_input.reshape(STRIPS, 1, ROWS, COLS, CIN),
    )


def solution(mesh):
    placed = (
        P(("dp", "tm", "space"), None, None, None),
        P(),
        P(),
        P(),
        P(("dp", "tm"), "space", None, None, None),
    )
    return jax.shard_map(
        local,
        mesh=mesh,
        in_specs=placed,
        out_specs=(
            P(("dp", "tm"), "space", None, None, None),
            P(("dp", "tm"), "space", None, None, None),
        ),
        check_vma=False,
    )
```

```python
import jax
import jax.numpy as jnp
from jax import lax
from jax.experimental import pallas as pl
from jax.experimental.pallas import tpu as pltpu
from jax.sharding import PartitionSpec as P

MESH = pl.DeviceIdType.MESH
F32 = jnp.float32
BF16 = jnp.bfloat16
EPS = 1e-06
STRIPS = 16
CHIPS = STRIPS // 2
ROWS = 4
COLS = 16
CIN = 512
COUT = 256
CELLS = STRIPS * ROWS * COLS
LINES = STRIPS * ROWS
PAD = 8
NT = (((1,), (1,)), ((), ()))


def activate(x, half_gain):
    inv = lax.rsqrt(jnp.mean(x * x, axis=-1, keepdims=True) + EPS)
    half = x * inv * half_gain
    return inv, half, 1.0 + jnp.tanh(half)


def mm(a, b):
    return jnp.dot(a, b, preferred_element_type=F32)


def kernel(
    lat, gain_hbm, w_hbm, sk_hbm, cot_hbm, w, acc, halo, gbuf,
    sk, gain, cot, arr, arrp, cotn, cedge, chalo, wide, grads, gh, gs, hid, pad, edge, stage,
    local_sem, own_sem, a_send, a_recv, c_send, c_recv, n_send, n_recv,
    h_send, h_recv, p_send, p_recv,
):
    me = lax.axis_index("space")
    tm = lax.axis_index("tm")
    chip = me // 2
    other = 1 - tm
    left, right = lax.rem(me + STRIPS - 1, STRIPS), lax.rem(me + 1, STRIPS)
    sides = ((0, right, COLS - 1), (1, left, 0))

    barrier = pltpu.get_barrier_semaphore()
    for k in range(1, STRIPS):
        pl.semaphore_signal(
            barrier, inc=1, device_id={"space": lax.rem(me + k, STRIPS)}, device_id_type=MESH
        )
    for s in (me, left, right):
        pl.semaphore_signal(
            barrier, inc=1, device_id={"space": s, "tm": other}, device_id_type=MESH
        )

    loads = [
        pltpu.make_async_copy(source, target, local_sem.at[i])
        for i, (source, target) in enumerate(
            ((cot_hbm, cot), (sk_hbm, sk), (gain_hbm, gain))
            + tuple((w_hbm.at[k], w.at[k]) for k in range(9))
        )
    ]
    for load in loads:
        load.start()
    own = pltpu.make_async_copy(
        lat.at[:, pl.ds(pl.multiple_of(me * COLS, COLS), COLS), :],
        arr.at[pl.ds(me * ROWS, ROWS)],
        own_sem,
    )
    own.start()

    loads[0].wait()
    wide[0:LINES, PAD : PAD + COLS] = cot[...].astype(F32)
    for slot, _, col in sides:
        cedge[slot] = wide[0:LINES, PAD + col, :].astype(BF16)

    pl.semaphore_wait(barrier, STRIPS - 1 + 3)

    started = []
    for slot, target, _ in sides:
        started.append(
            pltpu.make_async_remote_copy(
                src_ref=cedge.at[slot],
                dst_ref=chalo.at[slot, pl.ds(0, LINES)],
                send_sem=c_send.at[slot, 0],
                recv_sem=c_recv.at[slot, 0],
                device_id={"space": target},
                device_id_type=MESH,
            )
        )
        started.append(
            pltpu.make_async_remote_copy(
                src_ref=cedge.at[slot, pl.ds(0, 16)],
                dst_ref=chalo.at[slot, pl.ds(LINES, 16)],
                send_sem=c_send.at[slot, 1],
                recv_sem=c_recv.at[slot, 1],
                device_id={"space": target, "tm": other},
                device_id_type=MESH,
            )
        )
    started.append(
        pltpu.make_async_remote_copy(
            src_ref=cot.at[pl.ds(0, 2 * ROWS)],
            dst_ref=cotn,
            send_sem=n_send,
            recv_sem=n_recv,
            device_id={"tm": other},
            device_id_type=MESH,
        )
    )
    for copy in started:
        copy.start()

    def strip_copy(target, source, i):
        return pltpu.make_async_remote_copy(
            src_ref=lat.at[:, pl.ds(pl.multiple_of(target * COLS, COLS), COLS), :],
            dst_ref=arr.at[pl.ds(source * ROWS, ROWS)],
            send_sem=a_send.at[i],
            recv_sem=a_recv.at[source],
            device_id={"space": target},
            device_id_type=MESH,
        )

    def target_of(i):
        step = i // 2
        if i == 0:
            return chip * 2 + (1 - me % 2)
        step = (i + 1) // 2
        dist = (step + 1) // 2 * (1 if step % 2 else -1)
        return lax.rem(chip + dist + CHIPS, CHIPS) * 2 + lax.rem(me + i, 2)

    sends = [strip_copy(target_of(i), me, i) for i in range(STRIPS - 1)]
    for copy in sends:
        copy.start()

    hid[...] = jnp.zeros_like(hid)
    grads[...] = jnp.zeros_like(grads)
    pad[...] = jnp.zeros_like(pad)
    loads[1].wait()
    loads[2].wait()
    gs[...] = lax.dot_general(
        cot[...].reshape(CELLS, COUT), sk[...], NT, preferred_element_type=F32
    ).reshape(LINES, COLS, CIN)

    for copy in started:
        copy.wait_recv()
    first = jnp.where(tm == 0, 1.0, 0.0)
    second = 1.0 - first
    wide[LINES:, PAD : PAD + COLS] = cotn[...].astype(F32) * first
    has = (jnp.where(me > 0, 1.0, 0.0), jnp.where(me < STRIPS - 1, 1.0, 0.0))
    for slot, sublane in ((0, PAD - 1), (1, PAD + COLS)):
        wide[0:LINES, sublane, :] = chalo[slot, 0:LINES].astype(F32) * has[slot]
        after = chalo[slot, LINES : LINES + 16].astype(F32)[0:8]
        wide[LINES : LINES + 8, sublane, :] = after * (has[slot] * first)

    def spread(f, carry):
        lines = pl.ds(f * ROWS, ROWS)
        for tap in range(3):
            at = PAD + 1 - tap
            grads[f, 1 : 1 + ROWS, :, tap * COUT : (tap + 1) * COUT] = wide[
                lines, at : at + COLS
            ].astype(BF16)
        return carry

    lax.fori_loop(0, STRIPS + 2, spread, 0)

    gh[...] = jnp.zeros_like(gh)

    def backward(k, carry):
        t, h = k // 3, lax.rem(k, 3)
        pltpu.make_async_copy(w_hbm.at[k], w.at[k], local_sem.at[3 + k]).wait()
        part = jnp.zeros((CELLS, CIN), F32)
        for tap in range(3):
            window = grads[
                pl.ds(2 - t, STRIPS), pl.ds(2 - h, ROWS), :, tap * COUT : (tap + 1) * COUT
            ].reshape(CELLS, COUT)
            part = part + lax.dot_general(
                window, w[k, tap * CIN : (tap + 1) * CIN], NT, preferred_element_type=F32
            )
        gh[...] += part.reshape(LINES, COLS, CIN)
        return carry

    lax.fori_loop(0, 9, backward, 0)

    own.wait()

    def put_hidden(i, frame, hidden):
        wide_hidden = hidden.astype(F32).reshape(4, COLS, CIN)
        f = frame + i // 1
        rows = pl.ds(1 + 4 * lax.rem(i, 1), 4)
        pad[pl.ds(4 * i, 4), PAD : PAD + COLS] = wide_hidden
        hid[f, rows, :, CIN : 2 * CIN] = hidden.reshape(4, COLS, CIN)
        flat = hidden.astype(F32)
        col = lax.rem(lax.broadcasted_iota(jnp.int32, (4 * COLS, CIN), 0), COLS)
        low = jnp.where(col == 0, 0.0, pltpu.roll(flat, 1, 0))
        high = jnp.where(col == COLS - 1, 0.0, pltpu.roll(flat, 4 * COLS - 1, 0))
        hid[f, rows, :, 0:CIN] = low.astype(BF16).reshape(4, COLS, CIN)
        hid[f, rows, :, 2 * CIN :] = high.astype(BF16).reshape(4, COLS, CIN)

    def arrive(k, carry):
        step = (k + 1) // 2
        dist = jnp.where(lax.rem(k, 2) == 1, step, -step)
        c = lax.rem(chip + dist + CHIPS, CHIPS)
        for i in range(2):
            source = 2 * c + i

            @pl.when(source != me)
            def _():
                strip_copy(me, source, 0).wait_recv()

        def lines(i, carry):
            rows = pl.ds(c * 8 + 4 * i, 4)
            x = arr[rows].astype(F32).reshape(4 * COLS, CIN)
            half_gain = 0.5 * gain[...]
            inv, half, twice = activate(x, half_gain)
            hidden = half * twice
            put_hidden(i, c * 2 + 2, hidden.astype(BF16))
            gu = gh[rows].reshape(4 * COLS, CIN) * half_gain * (twice + hidden * (2.0 - twice))
            along = jnp.mean(gu * x, axis=-1, keepdims=True) * (inv * inv)
            gx = inv * (gu - x * along) + gs[rows].reshape(4 * COLS, CIN)
            gbuf[rows] = gx.astype(BF16).reshape(4, COLS, CIN)
            return carry

        lax.fori_loop(0, 2, lines, 0, unroll=2)
        for slot, target, col in sides:
            edge[slot, c] = pad[:, PAD + col, :]
            edge_copy(slot, target, c).start()
        return carry

    def edge_copy(slot, target, c):
        return pltpu.make_async_remote_copy(
            src_ref=edge.at[slot, c],
            dst_ref=halo.at[slot, pl.ds((c + 1) * 8, 8)],
            send_sem=h_send.at[slot, c],
            recv_sem=h_recv.at[slot, c],
            device_id={"space": target},
            device_id_type=MESH,
        )

    before = [
        pltpu.make_async_remote_copy(
            src_ref=arr.at[pl.ds(LINES - 8, 8)],
            dst_ref=arrp,
            send_sem=p_send.at[2],
            recv_sem=p_recv.at[2],
            device_id={"tm": other},
            device_id_type=MESH,
        )
    ]
    for slot, target, _ in sides:
        before.append(
            pltpu.make_async_remote_copy(
                src_ref=edge.at[slot, CHIPS - 1],
                dst_ref=halo.at[slot, pl.ds(0, 8)],
                send_sem=p_send.at[slot],
                recv_sem=p_recv.at[slot],
                device_id={"space": target, "tm": other},
                device_id_type=MESH,
            )
        )

    def forward(j, carry):
        lo = jnp.where(j == 0, 0, 2 * j + 1)
        hi = jnp.minimum(2 * j + 3, CHIPS)
        lax.fori_loop(lo, hi, arrive, 0)

        @pl.when(j == 3)
        def _():
            for copy in before:
                copy.start()

        c1 = lax.rem(chip - j + CHIPS, CHIPS)
        c2 = lax.rem(chip + j + 1, CHIPS)
        half = 2 * ROWS * COLS
        stage[0:half] = mm(arr[pl.ds(c1 * 8, 8)].reshape(half, CIN), sk[...])
        stage[half:] = mm(arr[pl.ds(c2 * 8, 8)].reshape(half, CIN), sk[...])

        def taps(t, carry):
            total = stage[...]
            for h in range(3):
                window = jnp.concatenate(
                    [hid[pl.ds(2 * c + t, 2), h : h + ROWS] for c in (c1, c2)], axis=0
                ).reshape(2 * half, 3 * CIN)
                total = total + mm(window, w[3 * t + h])
            stage[...] = total
            return carry

        lax.fori_loop(0, 3, taps, 0)
        acc[pl.ds(c1 * 8, 8)] = stage[0:half].reshape(8, COLS, COUT)
        acc[pl.ds(c2 * 8, 8)] = stage[half:].reshape(8, COLS, COUT)
        return carry

    lax.fori_loop(0, 4, forward, 0)

    before[0].wait_recv()

    def lines_before(i, carry):
        x = arrp[pl.ds(4 * i, 4)].astype(F32).reshape(4 * COLS, CIN)
        _, half, twice = activate(x, 0.5 * gain[...])
        put_hidden(i, 0, (half * twice * second).astype(BF16))
        return carry

    lax.fori_loop(0, 2, lines_before, 0)
    frame = ROWS * COLS
    both = acc[0 : 2 * ROWS].reshape(2 * frame, COUT)
    one = jnp.zeros((frame, COUT), F32)
    for h in range(3):
        both = both + mm(hid[0:2, h : h + ROWS].reshape(2 * frame, 3 * CIN), w[h])
        one = one + mm(hid[1, h : h + ROWS].reshape(frame, 3 * CIN), w[3 + h])
    acc[0 : 2 * ROWS] = both.reshape(2 * ROWS, COLS, COUT)
    acc[0:ROWS] += one.reshape(ROWS, COLS, COUT)

    for slot, target, _ in sides:

        def wait_edges(c, carry):
            edge_copy(slot, target, c).wait_recv()
            return carry

        lax.fori_loop(0, CHIPS, wait_edges, 0)
        before[1 + slot].wait_recv()
    for copy in sends + started + before:
        copy.wait_send()
    for slot, target, _ in sides:

        def wait_sent(c, carry):
            edge_copy(slot, target, c).wait_send()
            return carry

        lax.fori_loop(0, CHIPS, wait_sent, 0)


def finish(w, acc, halo, gbuf, out_hbm, gi_hbm, hrows, full, obuf, sem):
    ready = pltpu.make_async_copy(gbuf, gi_hbm, sem.at[0])
    ready.start()
    full[...] = acc[...]
    me = lax.axis_index("space")
    second = jnp.where(lax.axis_index("tm") == 0, 0.0, 1.0)
    has = (jnp.where(me > 0, 1.0, 0.0), jnp.where(me < STRIPS - 1, 1.0, 0.0))
    count = LINES + 8
    for slot, tap, col in ((0, 0, 0), (1, 2, COLS - 1)):
        row = lax.rem(lax.broadcasted_iota(jnp.int32, (count, CIN), 0), ROWS)
        line = lax.broadcasted_iota(jnp.int32, (count, CIN), 0)
        value = halo[slot] * (has[slot] * jnp.where(line < 8, second, 1.0))
        hrows[:, 0:CIN] = jnp.where(row == 0, 0.0, pltpu.roll(value, 1, 0))
        hrows[:, CIN : 2 * CIN] = value
        hrows[:, 2 * CIN :] = jnp.where(row == ROWS - 1, 0.0, pltpu.roll(value, count - 1, 0))
        total = jnp.zeros((LINES, COUT), F32)
        for t in range(3):
            window = hrows[t * ROWS : t * ROWS + LINES].astype(BF16)
            for h in range(3):
                total = total + mm(
                    window[:, h * CIN : (h + 1) * CIN],
                    w[3 * t + h, tap * CIN : (tap + 1) * CIN],
                )
        full[:, col, :] = full[:, col, :] + total

    obuf[...] = full[...].astype(BF16)
    result = pltpu.make_async_copy(obuf, out_hbm, sem.at[1])
    result.start()
    ready.wait()
    result.wait()


def local(latents, norm_gain, conv_weight, skip_weight, cotangent):
    hbm = pl.BlockSpec(memory_space=pl.ANY)
    dma = pltpu.SemaphoreType.DMA
    vmem = pl.BlockSpec(memory_space=pltpu.VMEM)
    parts = pl.pallas_call(
        kernel,
        out_shape=(
            pltpu.VMEM((9, 3 * CIN, COUT), BF16),
            pltpu.VMEM((LINES, COLS, COUT), F32),
            pltpu.VMEM((2, LINES + 8, CIN), F32),
            pltpu.VMEM((LINES, COLS, CIN), BF16),
        ),
        in_specs=[hbm] * 5,
        out_specs=(vmem,) * 4,
        scratch_shapes=[
            pltpu.VMEM((CIN, COUT), BF16),
            pltpu.VMEM((1, CIN), F32),
            pltpu.VMEM((LINES, COLS, COUT), BF16),
            pltpu.VMEM((LINES, COLS, CIN), BF16),
            pltpu.VMEM((8, COLS, CIN), BF16),
            pltpu.VMEM((8, COLS, COUT), BF16),
            pltpu.VMEM((2, LINES, COUT), BF16),
            pltpu.VMEM((2, LINES + 16, COUT), BF16),
            pltpu.VMEM((LINES + 8, 32, COUT), F32),
            pltpu.VMEM((STRIPS + 2, ROWS + 2, COLS, 3 * COUT), BF16),
            pltpu.VMEM((LINES, COLS, CIN), F32),
            pltpu.VMEM((LINES, COLS, CIN), F32),
            pltpu.VMEM((STRIPS + 2, ROWS + 2, COLS, 3 * CIN), BF16),
            pltpu.VMEM((8, 32, CIN), F32),
            pltpu.VMEM((2, CHIPS, 8, CIN), F32),
            pltpu.VMEM((4 * ROWS * COLS, COUT), F32),
            dma((3 + 9,)),
            dma,
            dma((STRIPS - 1,)),
            dma((STRIPS,)),
            dma((2, 2)),
            dma((2, 2)),
            dma,
            dma,
            dma((2, CHIPS)),
            dma((2, CHIPS)),
            dma((3,)),
            dma((3,)),
        ],
        compiler_params=pltpu.CompilerParams(
            collective_id=0, has_side_effects=True, vmem_limit_bytes=53 * 2**20
        ),
        cost_estimate=pl.CostEstimate(
            flops=2 * CELLS * CIN * COUT * 56, bytes_accessed=11 * 2**20, transcendentals=CELLS * CIN
        ),
    )(
        latents.reshape(ROWS, STRIPS * COLS, CIN),
        norm_gain.reshape(1, CIN),
        conv_weight.reshape(9, 3 * CIN, COUT),
        skip_weight,
        cotangent.reshape(LINES, COLS, COUT),
    )
    out, grad_input = pl.pallas_call(
        finish,
        out_shape=(
            jax.ShapeDtypeStruct((LINES, COLS, COUT), BF16),
            jax.ShapeDtypeStruct((LINES, COLS, CIN), BF16),
        ),
        in_specs=[vmem] * 4,
        out_specs=(hbm, hbm),
        scratch_shapes=[
            pltpu.VMEM((LINES + 8, 3 * CIN), F32),
            pltpu.VMEM((LINES, COLS, COUT), F32),
            pltpu.VMEM((LINES, COLS, COUT), BF16),
            dma((2,)),
        ],
        compiler_params=pltpu.CompilerParams(vmem_limit_bytes=16 * 2**20),
    )(*parts)
    return (
        out.reshape(STRIPS, 1, ROWS, COLS, COUT),
        grad_input.reshape(STRIPS, 1, ROWS, COLS, CIN),
    )


def solution(mesh):
    placed = (
        P(("dp", "tm", "space"), None, None, None),
        P(),
        P(),
        P(),
        P(("dp", "tm"), "space", None, None, None),
    )
    return jax.shard_map(
        local,
        mesh=mesh,
        in_specs=placed,
        out_specs=(
            P(("dp", "tm"), "space", None, None, None),
            P(("dp", "tm"), "space", None, None, None),
        ),
        check_vma=False,
    )
```

```python
import jax
import jax.numpy as jnp
from jax import lax
from jax.experimental import pallas as pl
from jax.experimental.pallas import tpu as pltpu
from jax.sharding import PartitionSpec as P

MESH = pl.DeviceIdType.MESH
F32 = jnp.float32
BF16 = jnp.bfloat16
EPS = 1e-06
STRIPS = 16
CHIPS = STRIPS // 2
ROWS = 4
COLS = 16
CIN = 512
COUT = 256
CELLS = STRIPS * ROWS * COLS
LINES = STRIPS * ROWS
PAD = 8
NT = (((1,), (1,)), ((), ()))


def activate(x, half_gain):
    inv = lax.rsqrt(jnp.mean(x * x, axis=-1, keepdims=True) + EPS)
    half = x * inv * half_gain
    return inv, half, 1.0 + jnp.tanh(half)


def mm(a, b):
    return jnp.dot(a, b, preferred_element_type=F32)


def put_hidden(hid, frame, hidden):
    count = hidden.shape[0] // (ROWS * COLS)
    rows = pl.ds(1, ROWS)
    frames = pl.ds(frame, count)
    shape = (count, ROWS, COLS, CIN)
    hid[frames, rows, :, CIN : 2 * CIN] = hidden.astype(BF16).reshape(shape)
    col = lax.rem(lax.broadcasted_iota(jnp.int32, hidden.shape, 0), COLS)
    low = jnp.where(col == 0, 0.0, pltpu.roll(hidden, 1, 0))
    high = jnp.where(col == COLS - 1, 0.0, pltpu.roll(hidden, hidden.shape[0] - 1, 0))
    hid[frames, rows, :, 0:CIN] = low.astype(BF16).reshape(shape)
    hid[frames, rows, :, 2 * CIN :] = high.astype(BF16).reshape(shape)


def kernel(
    lat, gain_hbm, w_hbm, sk_hbm, cot_hbm, w, acc, hidp, halo, gbuf,
    sk, gain, cot, arr, arrp, cotn, cedge, chalo, wide, grads, gh, gs, hid, pad, edge, edge_out,
    local_sem, own_sem, a_send, a_recv, c_send, c_recv, n_send, n_recv,
    h_send, h_recv, p_send, p_recv,
):
    me = lax.axis_index("space")
    tm = lax.axis_index("tm")
    chip = me // 2
    other = 1 - tm
    left, right = lax.rem(me + STRIPS - 1, STRIPS), lax.rem(me + 1, STRIPS)
    sides = ((0, right, COLS - 1), (1, left, 0))

    barrier = pltpu.get_barrier_semaphore()
    for k in range(1, STRIPS):
        pl.semaphore_signal(
            barrier, inc=1, device_id={"space": lax.rem(me + k, STRIPS)}, device_id_type=MESH
        )
    for s in (me, left, right):
        pl.semaphore_signal(
            barrier, inc=1, device_id={"space": s, "tm": other}, device_id_type=MESH
        )

    loads = [
        pltpu.make_async_copy(source, target, local_sem.at[i])
        for i, (source, target) in enumerate(
            ((cot_hbm, cot), (sk_hbm, sk), (gain_hbm, gain))
            + tuple((w_hbm.at[k], w.at[k]) for k in range(9))
        )
    ]
    for load in loads:
        load.start()
    own = pltpu.make_async_copy(
        lat.at[:, pl.ds(pl.multiple_of(me * COLS, COLS), COLS), :],
        arr.at[pl.ds(me * ROWS, ROWS)],
        own_sem,
    )
    own.start()

    loads[0].wait()
    wide[0:LINES, PAD : PAD + COLS] = cot[...].astype(F32)
    for slot, _, col in sides:
        cedge[slot] = wide[0:LINES, PAD + col, :].astype(BF16)

    pl.semaphore_wait(barrier, STRIPS - 1 + 3)

    started = []
    for slot, target, _ in sides:
        started.append(
            pltpu.make_async_remote_copy(
                src_ref=cedge.at[slot],
                dst_ref=chalo.at[slot, pl.ds(0, LINES)],
                send_sem=c_send.at[slot, 0],
                recv_sem=c_recv.at[slot, 0],
                device_id={"space": target},
                device_id_type=MESH,
            )
        )
        started.append(
            pltpu.make_async_remote_copy(
                src_ref=cedge.at[slot, pl.ds(0, 16)],
                dst_ref=chalo.at[slot, pl.ds(LINES, 16)],
                send_sem=c_send.at[slot, 1],
                recv_sem=c_recv.at[slot, 1],
                device_id={"space": target, "tm": other},
                device_id_type=MESH,
            )
        )
    started.append(
        pltpu.make_async_remote_copy(
            src_ref=cot.at[pl.ds(0, 2 * ROWS)],
            dst_ref=cotn,
            send_sem=n_send,
            recv_sem=n_recv,
            device_id={"tm": other},
            device_id_type=MESH,
        )
    )
    for copy in started:
        copy.start()

    def strip_copy(target, source, i):
        return pltpu.make_async_remote_copy(
            src_ref=lat.at[:, pl.ds(pl.multiple_of(target * COLS, COLS), COLS), :],
            dst_ref=arr.at[pl.ds(source * ROWS, ROWS)],
            send_sem=a_send.at[i],
            recv_sem=a_recv.at[source],
            device_id={"space": target},
            device_id_type=MESH,
        )

    def target_of(i):
        step = i // 2
        if i == 0:
            return chip * 2 + (1 - me % 2)
        step = (i + 1) // 2
        dist = (step + 1) // 2 * (1 if step % 2 else -1)
        return lax.rem(chip + dist + CHIPS, CHIPS) * 2 + lax.rem(me + i, 2)

    sends = [strip_copy(target_of(i), me, i) for i in range(STRIPS - 1)]
    for copy in sends:
        copy.start()

    for ref in (hid, grads, hidp):
        for r in (0, ROWS + 1):
            ref[:, r] = jnp.zeros((ref.shape[0],) + ref.shape[2:], BF16)
    acc[...] = jnp.zeros_like(acc)
    loads[1].wait()
    loads[2].wait()
    gs[...] = lax.dot_general(
        cot[...].reshape(CELLS, COUT), sk[...], NT, preferred_element_type=F32
    ).reshape(LINES, COLS, CIN)

    for copy in started:
        copy.wait_recv()
    first = jnp.where(tm == 0, 1.0, 0.0)
    wide[LINES:, PAD : PAD + COLS] = cotn[...].astype(F32) * first
    has = (jnp.where(me > 0, 1.0, 0.0), jnp.where(me < STRIPS - 1, 1.0, 0.0))
    for slot, sublane in ((0, PAD - 1), (1, PAD + COLS)):
        wide[0:LINES, sublane, :] = chalo[slot, 0:LINES].astype(F32) * has[slot]
        after = chalo[slot, LINES : LINES + 16].astype(F32)[0:8]
        wide[LINES : LINES + 8, sublane, :] = after * (has[slot] * first)

    def spread(f, carry):
        lines = pl.ds(f * ROWS, ROWS)
        for tap in range(3):
            at = PAD + 1 - tap
            grads[f, 1 : 1 + ROWS, :, tap * COUT : (tap + 1) * COUT] = wide[
                lines, at : at + COLS
            ].astype(BF16)
        return carry

    lax.fori_loop(0, STRIPS + 2, spread, 0)

    gh[...] = jnp.zeros_like(gh)

    def backward(k, carry):
        t, h = k // 3, lax.rem(k, 3)
        pltpu.make_async_copy(w_hbm.at[k], w.at[k], local_sem.at[3 + k]).wait()
        part = jnp.zeros((CELLS, CIN), F32)
        for tap in range(3):
            window = grads[
                pl.ds(2 - t, STRIPS), pl.ds(2 - h, ROWS), :, tap * COUT : (tap + 1) * COUT
            ].reshape(CELLS, COUT)
            part = part + lax.dot_general(
                window, w[k, tap * CIN : (tap + 1) * CIN], NT, preferred_element_type=F32
            )
        gh[...] += part.reshape(LINES, COLS, CIN)
        return carry

    lax.fori_loop(0, 9, backward, 0)

    own.wait()

    def chip_at(dist):
        return lax.rem(chip + dist + CHIPS, CHIPS)

    def await_chip(c):
        for i in range(2):
            source = 2 * c + i

            @pl.when(source != me)
            def _():
                strip_copy(me, source, 0).wait_recv()

    def arrive(c):
        half_gain = 0.5 * gain[...]
        for i in range(2):
            rows = pl.ds(c * 8 + ROWS * i, ROWS)
            x = arr[rows].astype(F32).reshape(ROWS * COLS, CIN)
            inv, half, twice = activate(x, half_gain)
            exact = half * twice
            hidden = exact.astype(BF16).astype(F32)
            pad[ROWS * i : ROWS * i + ROWS] = hidden.reshape(ROWS, COLS, CIN)
            put_hidden(hid, 2 * c + i, hidden)
            gu = gh[rows].reshape(ROWS * COLS, CIN) * half_gain * (twice + exact * (2.0 - twice))
            along = jnp.mean(gu * x, axis=-1, keepdims=True) * (inv * inv)
            gx = inv * (gu - x * along) + gs[rows].reshape(ROWS * COLS, CIN)
            gbuf[rows] = gx.astype(BF16).reshape(ROWS, COLS, CIN)
        for slot, _, col in sides:
            edge[slot, pl.ds(c * 8, 8)] = pad[:, col, :]

    half = 2 * ROWS * COLS

    def add(line, value):
        acc[pl.ds(line, 8)] += value.reshape(8, COLS, COUT)

    def forward(chips):
        def both(values):
            return values[0] if len(values) == 1 else jnp.concatenate(values, axis=0)

        shortcut = mm(both([arr[pl.ds(c * 8, 8)].reshape(half, CIN) for c in chips]), sk[...])
        for i, c in enumerate(chips):
            add(c * 8, shortcut[i * half : (i + 1) * half])

        def taps(t, carry):
            total = jnp.zeros((len(chips) * half, COUT), F32)
            for h in range(3):
                window = both(
                    [hid[pl.ds(2 * c, 2), h : h + ROWS].reshape(half, 3 * CIN) for c in chips]
                )
                total = total + mm(window, w[3 * t + h])
            for i, c in enumerate(chips):
                add((2 * c + 2 - t) * ROWS, total[i * half : (i + 1) * half])
            return carry

        lax.fori_loop(0, 3, taps, 0)

    before = [
        pltpu.make_async_remote_copy(
            src_ref=arr.at[pl.ds(LINES - 8, 8)],
            dst_ref=arrp,
            send_sem=p_send.at[2],
            recv_sem=p_recv.at[2],
            device_id={"tm": other},
            device_id_type=MESH,
        )
    ]
    columns = []
    for slot, target, _ in sides:
        columns.append(
            pltpu.make_async_remote_copy(
                src_ref=edge_out.at[slot],
                dst_ref=halo.at[slot, pl.ds(0, LINES)],
                send_sem=h_send.at[slot],
                recv_sem=h_recv.at[slot],
                device_id={"space": target},
                device_id_type=MESH,
            )
        )
        before.append(
            pltpu.make_async_remote_copy(
                src_ref=edge_out.at[slot, pl.ds(LINES - 16, 16)],
                dst_ref=halo.at[slot, pl.ds(LINES, 16)],
                send_sem=p_send.at[slot],
                recv_sem=p_recv.at[slot],
                device_id={"space": target, "tm": other},
                device_id_type=MESH,
            )
        )

    await_chip(chip)
    arrive(chip)
    forward([chip])

    def pair(j, carry):
        def one(i, carry):
            c = chip_at(jnp.where(i == 0, j, -j))
            await_chip(c)
            arrive(c)
            return carry

        lax.fori_loop(0, 2, one, 0)

        @pl.when(j < 3)
        def _():
            forward([chip_at(j), chip_at(-j)])

        return carry

    lax.fori_loop(1, 4, pair, 0)
    last = chip_at(4)
    await_chip(last)
    before[0].start()
    arrive(last)
    for slot in range(2):
        edge_out[slot] = edge[slot].astype(BF16)
    for copy in columns + before[1:]:
        copy.start()
    forward([chip_at(3), chip_at(-3), last])
    before[0].wait_recv()
    second = jnp.where(tm == 0, 0.0, 1.0)
    for i in range(2):
        x = arrp[ROWS * i : ROWS * i + ROWS].astype(F32).reshape(ROWS * COLS, CIN)
        _, value, twice = activate(x, 0.5 * gain[...])
        put_hidden(hidp, i, (value * twice).astype(BF16).astype(F32) * second)
    for copy in columns + before[1:]:
        copy.wait_recv()

    for copy in sends + started + columns + before:
        copy.wait_send()


def finish(w, acc, hidp, halo, gbuf, out_hbm, gi_hbm, hrows, full, obuf, sem):
    ready = pltpu.make_async_copy(gbuf, gi_hbm, sem.at[0])
    ready.start()
    me = lax.axis_index("space")
    second = jnp.where(lax.axis_index("tm") == 0, 0.0, 1.0)
    has = (jnp.where(me > 0, 1.0, 0.0), jnp.where(me < STRIPS - 1, 1.0, 0.0))
    full[...] = acc[0:LINES]

    count = LINES + 8
    line = lax.broadcasted_iota(jnp.int32, (count, CIN), 0)
    row = lax.rem(line, ROWS)
    for slot in range(2):
        got = halo[slot].astype(F32)
        value = jnp.concatenate([got[LINES + 8 :] * second, got[0:LINES]], axis=0) * has[slot]
        hrows[slot, :, 0:CIN] = jnp.where(row == 0, 0.0, pltpu.roll(value, 1, 0))
        hrows[slot, :, CIN : 2 * CIN] = value
        hrows[slot, :, 2 * CIN :] = jnp.where(
            row == ROWS - 1, 0.0, pltpu.roll(value, count - 1, 0)
        )

    frame = ROWS * COLS
    shares = [jnp.zeros((n, COUT), F32) for n in (2 * frame, frame, LINES, LINES)]
    for t in range(3):
        sides = [hrows[slot, t * ROWS : t * ROWS + LINES].astype(BF16) for slot in range(2)]
        for h in range(3):
            for c in range(3):
                takes = []
                if t < 2:
                    lines = hidp[t:2, h : h + ROWS, :, c * CIN : (c + 1) * CIN]
                    takes.append((t, lines.reshape((2 - t) * frame, CIN)))
                if c != 1:
                    takes.append((2 + c // 2, sides[c // 2][:, h * CIN : (h + 1) * CIN]))
                if not takes:
                    continue
                product = mm(
                    takes[0][1] if len(takes) == 1 else jnp.concatenate([v for _, v in takes], 0),
                    w[3 * t + h, c * CIN : (c + 1) * CIN],
                )
                start = 0
                for share, v in takes:
                    shares[share] = shares[share] + product[start : start + v.shape[0]]
                    start += v.shape[0]

    full[0:8] += shares[0].reshape(8, COLS, COUT)
    full[0:ROWS] += shares[1].reshape(ROWS, COLS, COUT)
    for col, share in ((0, shares[2]), (COLS - 1, shares[3])):
        full[:, col, :] = full[:, col, :] + share
    obuf[...] = full[...].astype(BF16)
    result = pltpu.make_async_copy(obuf, out_hbm, sem.at[1])
    result.start()
    ready.wait()
    result.wait()


def local(latents, norm_gain, conv_weight, skip_weight, cotangent):
    hbm = pl.BlockSpec(memory_space=pl.ANY)
    dma = pltpu.SemaphoreType.DMA
    vmem = pl.BlockSpec(memory_space=pltpu.VMEM)
    parts = pl.pallas_call(
        kernel,
        out_shape=(
            pltpu.VMEM((9, 3 * CIN, COUT), BF16),
            pltpu.VMEM((LINES + 8, COLS, COUT), F32),
            pltpu.VMEM((2, ROWS + 2, COLS, 3 * CIN), BF16),
            pltpu.VMEM((2, LINES + 16, CIN), BF16),
            pltpu.VMEM((LINES, COLS, CIN), BF16),
        ),
        in_specs=[hbm] * 5,
        out_specs=(vmem,) * 5,
        scratch_shapes=[
            pltpu.VMEM((CIN, COUT), BF16),
            pltpu.VMEM((1, CIN), F32),
            pltpu.VMEM((LINES, COLS, COUT), BF16),
            pltpu.VMEM((LINES, COLS, CIN), BF16),
            pltpu.VMEM((8, COLS, CIN), BF16),
            pltpu.VMEM((8, COLS, COUT), BF16),
            pltpu.VMEM((2, LINES, COUT), BF16),
            pltpu.VMEM((2, LINES + 16, COUT), BF16),
            pltpu.VMEM((LINES + 8, 32, COUT), F32),
            pltpu.VMEM((STRIPS + 2, ROWS + 2, COLS, 3 * COUT), BF16),
            pltpu.VMEM((LINES, COLS, CIN), F32),
            pltpu.VMEM((LINES, COLS, CIN), F32),
            pltpu.VMEM((STRIPS, ROWS + 2, COLS, 3 * CIN), BF16),
            pltpu.VMEM((8, COLS, CIN), F32),
            pltpu.VMEM((2, LINES, CIN), F32),
            pltpu.VMEM((2, LINES, CIN), BF16),
            dma((3 + 9,)),
            dma,
            dma((STRIPS - 1,)),
            dma((STRIPS,)),
            dma((2, 2)),
            dma((2, 2)),
            dma,
            dma,
            dma((2,)),
            dma((2,)),
            dma((3,)),
            dma((3,)),
        ],
        compiler_params=pltpu.CompilerParams(
            collective_id=0, has_side_effects=True, vmem_limit_bytes=53 * 2**20
        ),
        cost_estimate=pl.CostEstimate(
            flops=2 * CELLS * CIN * COUT * 56, bytes_accessed=11 * 2**20, transcendentals=CELLS * CIN
        ),
    )(
        latents.reshape(ROWS, STRIPS * COLS, CIN),
        norm_gain.reshape(1, CIN),
        conv_weight.reshape(9, 3 * CIN, COUT),
        skip_weight,
        cotangent.reshape(LINES, COLS, COUT),
    )
    out, grad_input = pl.pallas_call(
        finish,
        out_shape=(
            jax.ShapeDtypeStruct((LINES, COLS, COUT), BF16),
            jax.ShapeDtypeStruct((LINES, COLS, CIN), BF16),
        ),
        in_specs=[vmem] * 5,
        out_specs=(hbm, hbm),
        scratch_shapes=[
            pltpu.VMEM((2, LINES + 8, 3 * CIN), F32),
            pltpu.VMEM((LINES, COLS, COUT), F32),
            pltpu.VMEM((LINES, COLS, COUT), BF16),
            dma((2,)),
        ],
        compiler_params=pltpu.CompilerParams(vmem_limit_bytes=16 * 2**20),
    )(*parts)
    return (
        out.reshape(STRIPS, 1, ROWS, COLS, COUT),
        grad_input.reshape(STRIPS, 1, ROWS, COLS, CIN),
    )


def solution(mesh):
    placed = (
        P(("dp", "tm", "space"), None, None, None),
        P(),
        P(),
        P(),
        P(("dp", "tm"), "space", None, None, None),
    )
    return jax.shard_map(
        local,
        mesh=mesh,
        in_specs=placed,
        out_specs=(
            P(("dp", "tm"), "space", None, None, None),
            P(("dp", "tm"), "space", None, None, None),
        ),
        check_vma=False,
    )
```

```python
import jax
import jax.numpy as jnp
from jax import lax
from jax.experimental import pallas as pl
from jax.experimental.pallas import tpu as pltpu
from jax.sharding import PartitionSpec as P

MESH = pl.DeviceIdType.MESH
F32 = jnp.float32
BF16 = jnp.bfloat16
EPS = 1e-06
STRIPS = 16
CHIPS = STRIPS // 2
ROWS = 4
COLS = 16
CIN = 512
COUT = 256
CELLS = STRIPS * ROWS * COLS
LINES = STRIPS * ROWS
PAD = 8
NT = (((1,), (1,)), ((), ()))


def activate(x, half_gain):
    inv = lax.rsqrt(jnp.mean(x * x, axis=-1, keepdims=True) + EPS)
    half = x * inv * half_gain
    return inv, half, 1.0 + jnp.tanh(half)


def mm(a, b):
    return jnp.dot(a, b, preferred_element_type=F32)


def put_hidden(hid, frame, hidden):
    count = hidden.shape[0] // (ROWS * COLS)
    rows = pl.ds(1, ROWS)
    frames = pl.ds(frame, count)
    shape = (count, ROWS, COLS, CIN)
    hid[frames, rows, :, CIN : 2 * CIN] = hidden.astype(BF16).reshape(shape)
    col = lax.rem(lax.broadcasted_iota(jnp.int32, hidden.shape, 0), COLS)
    low = jnp.where(col == 0, 0.0, pltpu.roll(hidden, 1, 0))
    high = jnp.where(col == COLS - 1, 0.0, pltpu.roll(hidden, hidden.shape[0] - 1, 0))
    hid[frames, rows, :, 0:CIN] = low.astype(BF16).reshape(shape)
    hid[frames, rows, :, 2 * CIN :] = high.astype(BF16).reshape(shape)


def kernel(
    lat, gain_hbm, w_hbm, sk_hbm, cot_hbm, w, acc, hidp, halo, gbuf,
    sk, gain, cot, arr, arrp, cotn, cedge, chalo, wide, grads, gh, gs, hid, pad, edge, edge_out,
    local_sem, own_sem, a_send, a_recv, c_send, c_recv, n_send, n_recv,
    h_send, h_recv, p_send, p_recv,
):
    me = lax.axis_index("space")
    tm = lax.axis_index("tm")
    chip = me // 2
    other = 1 - tm
    left, right = lax.rem(me + STRIPS - 1, STRIPS), lax.rem(me + 1, STRIPS)
    sides = ((0, right, COLS - 1), (1, left, 0))

    barrier = pltpu.get_barrier_semaphore()
    for k in (8, 7, 9, 6, 10, 5, 11, 4, 12, 3, 13, 2, 14, 1, 15):
        pl.semaphore_signal(
            barrier, inc=1, device_id={"space": lax.rem(me + k, STRIPS)}, device_id_type=MESH
        )
    for s in (me, left, right):
        pl.semaphore_signal(
            barrier, inc=1, device_id={"space": s, "tm": other}, device_id_type=MESH
        )

    loads = [
        pltpu.make_async_copy(source, target, local_sem.at[i])
        for i, (source, target) in enumerate(
            ((cot_hbm, cot), (sk_hbm, sk), (gain_hbm, gain))
            + tuple((w_hbm.at[k], w.at[k]) for k in range(9))
        )
    ]
    for load in loads:
        load.start()
    own = pltpu.make_async_copy(
        lat.at[:, pl.ds(pl.multiple_of(me * COLS, COLS), COLS), :],
        arr.at[pl.ds(me * ROWS, ROWS)],
        own_sem,
    )
    own.start()

    loads[0].wait()
    wide[0:LINES, PAD : PAD + COLS] = cot[...].astype(F32)
    for slot, _, col in sides:
        cedge[slot] = wide[0:LINES, PAD + col, :].astype(BF16)

    pl.semaphore_wait(barrier, STRIPS - 1 + 3)

    started = []
    for slot, target, _ in sides:
        started.append(
            pltpu.make_async_remote_copy(
                src_ref=cedge.at[slot],
                dst_ref=chalo.at[slot, pl.ds(0, LINES)],
                send_sem=c_send.at[slot, 0],
                recv_sem=c_recv.at[slot, 0],
                device_id={"space": target},
                device_id_type=MESH,
            )
        )
        started.append(
            pltpu.make_async_remote_copy(
                src_ref=cedge.at[slot, pl.ds(0, 16)],
                dst_ref=chalo.at[slot, pl.ds(LINES, 16)],
                send_sem=c_send.at[slot, 1],
                recv_sem=c_recv.at[slot, 1],
                device_id={"space": target, "tm": other},
                device_id_type=MESH,
            )
        )
    started.append(
        pltpu.make_async_remote_copy(
            src_ref=cot.at[pl.ds(0, 2 * ROWS)],
            dst_ref=cotn,
            send_sem=n_send,
            recv_sem=n_recv,
            device_id={"tm": other},
            device_id_type=MESH,
        )
    )
    for copy in started:
        copy.start()

    def strip_copy(target, source, i):
        return pltpu.make_async_remote_copy(
            src_ref=lat.at[:, pl.ds(pl.multiple_of(target * COLS, COLS), COLS), :],
            dst_ref=arr.at[pl.ds(source * ROWS, ROWS)],
            send_sem=a_send.at[i],
            recv_sem=a_recv.at[source],
            device_id={"space": target},
            device_id_type=MESH,
        )

    def target_of(i):
        step = i // 2
        if i == 0:
            return chip * 2 + (1 - me % 2)
        step = (i + 1) // 2
        dist = (step + 1) // 2 * (1 if step % 2 else -1)
        return lax.rem(chip + dist + CHIPS, CHIPS) * 2 + lax.rem(me + i, 2)

    sends = [strip_copy(target_of(i), me, i) for i in range(STRIPS - 1)]
    for copy in sends:
        copy.start()

    for ref in (hid, grads, hidp):
        for r in (0, ROWS + 1):
            ref[:, r] = jnp.zeros((ref.shape[0],) + ref.shape[2:], BF16)
    acc[...] = jnp.zeros_like(acc)
    loads[1].wait()
    loads[2].wait()
    gs[...] = lax.dot_general(
        cot[...].reshape(CELLS, COUT), sk[...], NT, preferred_element_type=F32
    ).reshape(LINES, COLS, CIN)

    for copy in started:
        copy.wait_recv()
    first = jnp.where(tm == 0, 1.0, 0.0)
    wide[LINES:, PAD : PAD + COLS] = cotn[...].astype(F32) * first
    has = (jnp.where(me > 0, 1.0, 0.0), jnp.where(me < STRIPS - 1, 1.0, 0.0))
    for slot, sublane in ((0, PAD - 1), (1, PAD + COLS)):
        wide[0:LINES, sublane, :] = chalo[slot, 0:LINES].astype(F32) * has[slot]
        after = chalo[slot, LINES : LINES + 16].astype(F32)[0:8]
        wide[LINES : LINES + 8, sublane, :] = after * (has[slot] * first)

    def spread(f, carry):
        lines = pl.ds(f * ROWS, ROWS)
        for tap in range(3):
            at = PAD + 1 - tap
            grads[f, 1 : 1 + ROWS, :, tap * COUT : (tap + 1) * COUT] = wide[
                lines, at : at + COLS
            ].astype(BF16)
        return carry

    lax.fori_loop(0, STRIPS + 2, spread, 0)

    gh[...] = jnp.zeros_like(gh)

    def backward(k, carry):
        t, h = k // 3, lax.rem(k, 3)
        pltpu.make_async_copy(w_hbm.at[k], w.at[k], local_sem.at[3 + k]).wait()
        part = jnp.zeros((CELLS, CIN), F32)
        for tap in range(3):
            window = grads[
                pl.ds(2 - t, STRIPS), pl.ds(2 - h, ROWS), :, tap * COUT : (tap + 1) * COUT
            ].reshape(CELLS, COUT)
            part = part + lax.dot_general(
                window, w[k, tap * CIN : (tap + 1) * CIN], NT, preferred_element_type=F32
            )
        gh[...] += part.reshape(LINES, COLS, CIN)
        return carry

    lax.fori_loop(0, 9, backward, 0)

    own.wait()

    def chip_at(dist):
        return lax.rem(chip + dist + CHIPS, CHIPS)

    def await_chip(c):
        for i in range(2):
            source = 2 * c + i

            @pl.when(source != me)
            def _():
                strip_copy(me, source, 0).wait_recv()

    def arrive(c, grad=True):
        half_gain = 0.5 * gain[...]
        for i in range(2):
            rows = pl.ds(c * 8 + ROWS * i, ROWS)
            x = arr[rows].astype(F32).reshape(ROWS * COLS, CIN)
            inv, half, twice = activate(x, half_gain)
            exact = half * twice
            hidden = exact.astype(BF16).astype(F32)
            pad[ROWS * i : ROWS * i + ROWS] = hidden.reshape(ROWS, COLS, CIN)
            put_hidden(hid, 2 * c + i, hidden)
            if grad:
                gradient(rows, x, inv, half_gain, twice, exact)
        for slot, _, col in sides:
            edge[slot, pl.ds(c * 8, 8)] = pad[:, col, :]

    def gradient(rows, x, inv, half_gain, twice, exact):
        gu = gh[rows].reshape(ROWS * COLS, CIN) * half_gain * (twice + exact * (2.0 - twice))
        along = jnp.mean(gu * x, axis=-1, keepdims=True) * (inv * inv)
        gx = inv * (gu - x * along) + gs[rows].reshape(ROWS * COLS, CIN)
        gbuf[rows] = gx.astype(BF16).reshape(ROWS, COLS, CIN)

    def late_gradient(c):
        half_gain = 0.5 * gain[...]
        for i in range(2):
            rows = pl.ds(c * 8 + ROWS * i, ROWS)
            x = arr[rows].astype(F32).reshape(ROWS * COLS, CIN)
            inv, half, twice = activate(x, half_gain)
            gradient(rows, x, inv, half_gain, twice, half * twice)

    half = 2 * ROWS * COLS

    def add(line, value):
        acc[pl.ds(line, 8)] += value.reshape(8, COLS, COUT)

    def forward(chips):
        def both(values):
            return values[0] if len(values) == 1 else jnp.concatenate(values, axis=0)

        shortcut = mm(both([arr[pl.ds(c * 8, 8)].reshape(half, CIN) for c in chips]), sk[...])
        for i, c in enumerate(chips):
            add(c * 8, shortcut[i * half : (i + 1) * half])

        def taps(t, carry):
            total = jnp.zeros((len(chips) * half, COUT), F32)
            for h in range(3):
                window = both(
                    [hid[pl.ds(2 * c, 2), h : h + ROWS].reshape(half, 3 * CIN) for c in chips]
                )
                total = total + mm(window, w[3 * t + h])
            for i, c in enumerate(chips):
                add((2 * c + 2 - t) * ROWS, total[i * half : (i + 1) * half])
            return carry

        lax.fori_loop(0, 3, taps, 0)

    before = [
        pltpu.make_async_remote_copy(
            src_ref=arr.at[pl.ds(LINES - 8, 8)],
            dst_ref=arrp,
            send_sem=p_send.at[2],
            recv_sem=p_recv.at[2],
            device_id={"tm": other},
            device_id_type=MESH,
        )
    ]
    columns = []
    for slot, target, _ in sides:
        columns.append(
            pltpu.make_async_remote_copy(
                src_ref=edge_out.at[slot],
                dst_ref=halo.at[slot, pl.ds(0, LINES)],
                send_sem=h_send.at[slot],
                recv_sem=h_recv.at[slot],
                device_id={"space": target},
                device_id_type=MESH,
            )
        )
        before.append(
            pltpu.make_async_remote_copy(
                src_ref=edge_out.at[slot, pl.ds(LINES - 16, 16)],
                dst_ref=halo.at[slot, pl.ds(LINES, 16)],
                send_sem=p_send.at[slot],
                recv_sem=p_recv.at[slot],
                device_id={"space": target, "tm": other},
                device_id_type=MESH,
            )
        )

    await_chip(chip)
    arrive(chip)
    forward([chip])

    def pair(j, carry):
        def one(i, carry):
            c = chip_at(jnp.where(i == 0, j, -j))
            await_chip(c)
            arrive(c)
            return carry

        lax.fori_loop(0, 2, one, 0)

        @pl.when(j < 3)
        def _():
            forward([chip_at(j), chip_at(-j)])

        return carry

    lax.fori_loop(1, 4, pair, 0)
    last = chip_at(4)
    await_chip(last)
    before[0].start()
    arrive(last, grad=False)
    for slot in range(2):
        edge_out[slot] = edge[slot].astype(BF16)
    for copy in columns + before[1:]:
        copy.start()
    late_gradient(last)
    forward([chip_at(3), chip_at(-3), last])
    before[0].wait_recv()
    second = jnp.where(tm == 0, 0.0, 1.0)
    for i in range(2):
        x = arrp[ROWS * i : ROWS * i + ROWS].astype(F32).reshape(ROWS * COLS, CIN)
        _, value, twice = activate(x, 0.5 * gain[...])
        put_hidden(hidp, i, (value * twice).astype(BF16).astype(F32) * second)
    for copy in columns + before[1:]:
        copy.wait_recv()

    for copy in sends + started + columns + before:
        copy.wait_send()


def finish(w, acc, hidp, halo, gbuf, out_hbm, gi_hbm, hrows, full, obuf, sem):
    ready = pltpu.make_async_copy(gbuf, gi_hbm, sem.at[0])
    ready.start()
    me = lax.axis_index("space")
    second = jnp.where(lax.axis_index("tm") == 0, 0.0, 1.0)
    has = (jnp.where(me > 0, 1.0, 0.0), jnp.where(me < STRIPS - 1, 1.0, 0.0))
    full[...] = acc[0:LINES]

    count = LINES + 8
    line = lax.broadcasted_iota(jnp.int32, (count, CIN), 0)
    row = lax.rem(line, ROWS)
    for slot in range(2):
        got = halo[slot].astype(F32)
        value = jnp.concatenate([got[LINES + 8 :] * second, got[0:LINES]], axis=0) * has[slot]
        hrows[slot, :, 0:CIN] = jnp.where(row == 0, 0.0, pltpu.roll(value, 1, 0))
        hrows[slot, :, CIN : 2 * CIN] = value
        hrows[slot, :, 2 * CIN :] = jnp.where(
            row == ROWS - 1, 0.0, pltpu.roll(value, count - 1, 0)
        )

    frame = ROWS * COLS
    shares = [jnp.zeros((n, COUT), F32) for n in (2 * frame, frame, LINES, LINES)]
    for t in range(3):
        sides = [hrows[slot, t * ROWS : t * ROWS + LINES].astype(BF16) for slot in range(2)]
        for h in range(3):
            for c in range(3):
                takes = []
                if t < 2:
                    lines = hidp[t:2, h : h + ROWS, :, c * CIN : (c + 1) * CIN]
                    takes.append((t, lines.reshape((2 - t) * frame, CIN)))
                if c != 1:
                    takes.append((2 + c // 2, sides[c // 2][:, h * CIN : (h + 1) * CIN]))
                if not takes:
                    continue
                product = mm(
                    takes[0][1] if len(takes) == 1 else jnp.concatenate([v for _, v in takes], 0),
                    w[3 * t + h, c * CIN : (c + 1) * CIN],
                )
                start = 0
                for share, v in takes:
                    shares[share] = shares[share] + product[start : start + v.shape[0]]
                    start += v.shape[0]

    full[0:8] += shares[0].reshape(8, COLS, COUT)
    full[0:ROWS] += shares[1].reshape(ROWS, COLS, COUT)
    for col, share in ((0, shares[2]), (COLS - 1, shares[3])):
        full[:, col, :] = full[:, col, :] + share
    obuf[...] = full[...].astype(BF16)
    result = pltpu.make_async_copy(obuf, out_hbm, sem.at[1])
    result.start()
    ready.wait()
    result.wait()


def local(latents, norm_gain, conv_weight, skip_weight, cotangent):
    hbm = pl.BlockSpec(memory_space=pl.ANY)
    dma = pltpu.SemaphoreType.DMA
    vmem = pl.BlockSpec(memory_space=pltpu.VMEM)
    parts = pl.pallas_call(
        kernel,
        out_shape=(
            pltpu.VMEM((9, 3 * CIN, COUT), BF16),
            pltpu.VMEM((LINES + 8, COLS, COUT), F32),
            pltpu.VMEM((2, ROWS + 2, COLS, 3 * CIN), BF16),
            pltpu.VMEM((2, LINES + 16, CIN), BF16),
            pltpu.VMEM((LINES, COLS, CIN), BF16),
        ),
        in_specs=[hbm] * 5,
        out_specs=(vmem,) * 5,
        scratch_shapes=[
            pltpu.VMEM((CIN, COUT), BF16),
            pltpu.VMEM((1, CIN), F32),
            pltpu.VMEM((LINES, COLS, COUT), BF16),
            pltpu.VMEM((LINES, COLS, CIN), BF16),
            pltpu.VMEM((8, COLS, CIN), BF16),
            pltpu.VMEM((8, COLS, COUT), BF16),
            pltpu.VMEM((2, LINES, COUT), BF16),
            pltpu.VMEM((2, LINES + 16, COUT), BF16),
            pltpu.VMEM((LINES + 8, 32, COUT), F32),
            pltpu.VMEM((STRIPS + 2, ROWS + 2, COLS, 3 * COUT), BF16),
            pltpu.VMEM((LINES, COLS, CIN), F32),
            pltpu.VMEM((LINES, COLS, CIN), F32),
            pltpu.VMEM((STRIPS, ROWS + 2, COLS, 3 * CIN), BF16),
            pltpu.VMEM((8, COLS, CIN), F32),
            pltpu.VMEM((2, LINES, CIN), F32),
            pltpu.VMEM((2, LINES, CIN), BF16),
            dma((3 + 9,)),
            dma,
            dma((STRIPS - 1,)),
            dma((STRIPS,)),
            dma((2, 2)),
            dma((2, 2)),
            dma,
            dma,
            dma((2,)),
            dma((2,)),
            dma((3,)),
            dma((3,)),
        ],
        compiler_params=pltpu.CompilerParams(
            collective_id=0, has_side_effects=True, vmem_limit_bytes=53 * 2**20
        ),
        cost_estimate=pl.CostEstimate(
            flops=2 * CELLS * CIN * COUT * 56, bytes_accessed=11 * 2**20, transcendentals=CELLS * CIN
        ),
    )(
        latents.reshape(ROWS, STRIPS * COLS, CIN),
        norm_gain.reshape(1, CIN),
        conv_weight.reshape(9, 3 * CIN, COUT),
        skip_weight,
        cotangent.reshape(LINES, COLS, COUT),
    )
    out, grad_input = pl.pallas_call(
        finish,
        out_shape=(
            jax.ShapeDtypeStruct((LINES, COLS, COUT), BF16),
            jax.ShapeDtypeStruct((LINES, COLS, CIN), BF16),
        ),
        in_specs=[vmem] * 5,
        out_specs=(hbm, hbm),
        scratch_shapes=[
            pltpu.VMEM((2, LINES + 8, 3 * CIN), F32),
            pltpu.VMEM((LINES, COLS, COUT), F32),
            pltpu.VMEM((LINES, COLS, COUT), BF16),
            dma((2,)),
        ],
        compiler_params=pltpu.CompilerParams(vmem_limit_bytes=16 * 2**20),
    )(*parts)
    return (
        out.reshape(STRIPS, 1, ROWS, COLS, COUT),
        grad_input.reshape(STRIPS, 1, ROWS, COLS, CIN),
    )


def solution(mesh):
    placed = (
        P(("dp", "tm", "space"), None, None, None),
        P(),
        P(),
        P(),
        P(("dp", "tm"), "space", None, None, None),
    )
    return jax.shard_map(
        local,
        mesh=mesh,
        in_specs=placed,
        out_specs=(
            P(("dp", "tm"), "space", None, None, None),
            P(("dp", "tm"), "space", None, None, None),
        ),
        check_vma=False,
    )
```

```python
import jax
import jax.numpy as jnp
from jax import lax
from jax.experimental import pallas as pl
from jax.experimental.pallas import tpu as pltpu
from jax.sharding import PartitionSpec as P

MESH = pl.DeviceIdType.MESH
F32 = jnp.float32
BF16 = jnp.bfloat16
EPS = 1e-06
STRIPS = 16
CHIPS = STRIPS // 2
ROWS = 4
COLS = 16
CIN = 512
COUT = 256
CELLS = STRIPS * ROWS * COLS
LINES = STRIPS * ROWS
PAD = 8
NT = (((1,), (1,)), ((), ()))


def activate(x, half_gain):
    inv = lax.rsqrt(jnp.mean(x * x, axis=-1, keepdims=True) + EPS)
    half = x * inv * half_gain
    return inv, half, 1.0 + jnp.tanh(half)


def mm(a, b):
    return jnp.dot(a, b, preferred_element_type=F32)


def put_hidden(hid, frame, hidden):
    count = hidden.shape[0] // (ROWS * COLS)
    rows = pl.ds(1, ROWS)
    frames = pl.ds(frame, count)
    shape = (count, ROWS, COLS, CIN)
    hid[frames, rows, :, CIN : 2 * CIN] = hidden.astype(BF16).reshape(shape)
    col = lax.rem(lax.broadcasted_iota(jnp.int32, hidden.shape, 0), COLS)
    low = jnp.where(col == 0, 0.0, pltpu.roll(hidden, 1, 0))
    high = jnp.where(col == COLS - 1, 0.0, pltpu.roll(hidden, hidden.shape[0] - 1, 0))
    hid[frames, rows, :, 0:CIN] = low.astype(BF16).reshape(shape)
    hid[frames, rows, :, 2 * CIN :] = high.astype(BF16).reshape(shape)


def kernel(
    lat, gain_hbm, w_hbm, sk_hbm, cot_hbm, w, acc, hidp, halo, gbuf,
    sk, gain, cot, arr, arrp, cotn, cedge, chalo, wide, grads, gh, gs, hid, pad, edge, edge_out,
    local_sem, own_sem, a_send, a_recv, c_send, c_recv, n_send, n_recv,
    h_send, h_recv, p_send, p_recv,
):
    me = lax.axis_index("space")
    tm = lax.axis_index("tm")
    chip = me // 2
    other = 1 - tm
    left, right = lax.rem(me + STRIPS - 1, STRIPS), lax.rem(me + 1, STRIPS)
    sides = ((0, right, COLS - 1), (1, left, 0))

    barrier = pltpu.get_barrier_semaphore()
    for k in (8, 7, 9, 6, 10, 5, 11, 4, 12, 3, 13, 2, 14, 1, 15):
        pl.semaphore_signal(
            barrier, inc=1, device_id={"space": lax.rem(me + k, STRIPS)}, device_id_type=MESH
        )
    for s in (me, left, right):
        pl.semaphore_signal(
            barrier, inc=1, device_id={"space": s, "tm": other}, device_id_type=MESH
        )

    loads = [
        pltpu.make_async_copy(source, target, local_sem.at[i])
        for i, (source, target) in enumerate(
            ((cot_hbm, cot), (sk_hbm, sk), (gain_hbm, gain))
            + tuple((w_hbm.at[k], w.at[k]) for k in range(9))
        )
    ]
    for load in loads:
        load.start()
    own = pltpu.make_async_copy(
        lat.at[:, pl.ds(pl.multiple_of(me * COLS, COLS), COLS), :],
        arr.at[pl.ds(me * ROWS, ROWS)],
        own_sem,
    )
    own.start()

    loads[0].wait()
    wide[0:LINES, PAD : PAD + COLS] = cot[...].astype(F32)
    for slot, _, col in sides:
        cedge[slot] = wide[0:LINES, PAD + col, :].astype(BF16)

    pl.semaphore_wait(barrier, STRIPS - 1 + 3)

    started = []
    for slot, target, _ in sides:
        started.append(
            pltpu.make_async_remote_copy(
                src_ref=cedge.at[slot],
                dst_ref=chalo.at[slot, pl.ds(0, LINES)],
                send_sem=c_send.at[slot, 0],
                recv_sem=c_recv.at[slot, 0],
                device_id={"space": target},
                device_id_type=MESH,
            )
        )
        started.append(
            pltpu.make_async_remote_copy(
                src_ref=cedge.at[slot, pl.ds(0, 16)],
                dst_ref=chalo.at[slot, pl.ds(LINES, 16)],
                send_sem=c_send.at[slot, 1],
                recv_sem=c_recv.at[slot, 1],
                device_id={"space": target, "tm": other},
                device_id_type=MESH,
            )
        )
    started.append(
        pltpu.make_async_remote_copy(
            src_ref=cot.at[pl.ds(0, 2 * ROWS)],
            dst_ref=cotn,
            send_sem=n_send,
            recv_sem=n_recv,
            device_id={"tm": other},
            device_id_type=MESH,
        )
    )
    for copy in started:
        copy.start()

    def strip_copy(target, source, i):
        return pltpu.make_async_remote_copy(
            src_ref=lat.at[:, pl.ds(pl.multiple_of(target * COLS, COLS), COLS), :],
            dst_ref=arr.at[pl.ds(source * ROWS, ROWS)],
            send_sem=a_send.at[i],
            recv_sem=a_recv.at[source],
            device_id={"space": target},
            device_id_type=MESH,
        )

    def target_of(i):
        step = i // 2
        if i == 0:
            return chip * 2 + (1 - me % 2)
        step = (i + 1) // 2
        dist = (step + 1) // 2 * (1 if step % 2 else -1)
        return lax.rem(chip + dist + CHIPS, CHIPS) * 2 + lax.rem(me + i, 2)

    sends = [strip_copy(target_of(i), me, i) for i in range(STRIPS - 1)]
    for copy in sends:
        copy.start()

    for ref in (hid, grads, hidp):
        for r in (0, ROWS + 1):
            ref[:, r] = jnp.zeros((ref.shape[0],) + ref.shape[2:], BF16)
    acc[...] = jnp.zeros_like(acc)
    loads[1].wait()
    loads[2].wait()
    gs[...] = lax.dot_general(
        cot[...].reshape(CELLS, COUT), sk[...], NT, preferred_element_type=F32
    ).reshape(LINES, COLS, CIN)

    for copy in started:
        copy.wait_recv()
    first = jnp.where(tm == 0, 1.0, 0.0)
    wide[LINES:, PAD : PAD + COLS] = cotn[...].astype(F32) * first
    has = (jnp.where(me > 0, 1.0, 0.0), jnp.where(me < STRIPS - 1, 1.0, 0.0))
    for slot, sublane in ((0, PAD - 1), (1, PAD + COLS)):
        wide[0:LINES, sublane, :] = chalo[slot, 0:LINES].astype(F32) * has[slot]
        after = chalo[slot, LINES : LINES + 16].astype(F32)[0:8]
        wide[LINES : LINES + 8, sublane, :] = after * (has[slot] * first)

    def spread(f, carry):
        lines = pl.ds(f * ROWS, ROWS)
        for tap in range(3):
            at = PAD + 1 - tap
            grads[f, 1 : 1 + ROWS, :, tap * COUT : (tap + 1) * COUT] = wide[
                lines, at : at + COLS
            ].astype(BF16)
        return carry

    lax.fori_loop(0, STRIPS + 2, spread, 0)

    gh[...] = jnp.zeros_like(gh)

    def backward(k, carry):
        t, h = k // 3, lax.rem(k, 3)
        pltpu.make_async_copy(w_hbm.at[k], w.at[k], local_sem.at[3 + k]).wait()
        part = jnp.zeros((CELLS, CIN), F32)
        for tap in range(3):
            window = grads[
                pl.ds(2 - t, STRIPS), pl.ds(2 - h, ROWS), :, tap * COUT : (tap + 1) * COUT
            ].reshape(CELLS, COUT)
            part = part + lax.dot_general(
                window, w[k, tap * CIN : (tap + 1) * CIN], NT, preferred_element_type=F32
            )
        gh[...] += part.reshape(LINES, COLS, CIN)
        return carry

    lax.fori_loop(0, 9, backward, 0)

    own.wait()

    def chip_at(dist):
        return lax.rem(chip + dist + CHIPS, CHIPS)

    def await_chip(c):
        for i in range(2):
            source = 2 * c + i

            @pl.when(source != me)
            def _():
                strip_copy(me, source, 0).wait_recv()

    def arrive(c, grad=True):
        half_gain = 0.5 * gain[...]
        for i in range(2):
            rows = pl.ds(c * 8 + ROWS * i, ROWS)
            x = arr[rows].astype(F32).reshape(ROWS * COLS, CIN)
            inv, half, twice = activate(x, half_gain)
            exact = half * twice
            hidden = exact.astype(BF16).astype(F32)
            pad[ROWS * i : ROWS * i + ROWS] = hidden.reshape(ROWS, COLS, CIN)
            put_hidden(hid, 2 * c + i, hidden)
            if grad:
                gradient(rows, x, inv, half_gain, twice, exact)
        for slot, _, col in sides:
            edge[slot, pl.ds(c * 8, 8)] = pad[:, col, :]

    def gradient(rows, x, inv, half_gain, twice, exact):
        gu = gh[rows].reshape(ROWS * COLS, CIN) * half_gain * (twice + exact * (2.0 - twice))
        along = jnp.mean(gu * x, axis=-1, keepdims=True) * (inv * inv)
        gx = inv * (gu - x * along) + gs[rows].reshape(ROWS * COLS, CIN)
        gbuf[rows] = gx.astype(BF16).reshape(ROWS, COLS, CIN)

    def late_gradient(c):
        half_gain = 0.5 * gain[...]
        for i in range(2):
            rows = pl.ds(c * 8 + ROWS * i, ROWS)
            x = arr[rows].astype(F32).reshape(ROWS * COLS, CIN)
            inv, half, twice = activate(x, half_gain)
            gradient(rows, x, inv, half_gain, twice, half * twice)

    half = 2 * ROWS * COLS

    def add(line, value):
        acc[pl.ds(line, 8)] += value.reshape(8, COLS, COUT)

    def forward(chips):
        def both(values):
            return values[0] if len(values) == 1 else jnp.concatenate(values, axis=0)

        shortcut = mm(both([arr[pl.ds(c * 8, 8)].reshape(half, CIN) for c in chips]), sk[...])
        for i, c in enumerate(chips):
            add(c * 8, shortcut[i * half : (i + 1) * half])

        def taps(t, carry):
            total = jnp.zeros((len(chips) * half, COUT), F32)
            for h in range(3):
                window = both(
                    [hid[pl.ds(2 * c, 2), h : h + ROWS].reshape(half, 3 * CIN) for c in chips]
                )
                total = total + mm(window, w[3 * t + h])
            for i, c in enumerate(chips):
                add((2 * c + 2 - t) * ROWS, total[i * half : (i + 1) * half])
            return carry

        lax.fori_loop(0, 3, taps, 0)

    before = [
        pltpu.make_async_remote_copy(
            src_ref=arr.at[pl.ds(LINES - 8, 8)],
            dst_ref=arrp,
            send_sem=p_send.at[2],
            recv_sem=p_recv.at[2],
            device_id={"tm": other},
            device_id_type=MESH,
        )
    ]
    columns = []
    for slot, target, _ in sides:
        columns.append(
            pltpu.make_async_remote_copy(
                src_ref=edge_out.at[slot],
                dst_ref=halo.at[slot, pl.ds(0, LINES)],
                send_sem=h_send.at[slot],
                recv_sem=h_recv.at[slot],
                device_id={"space": target},
                device_id_type=MESH,
            )
        )
        before.append(
            pltpu.make_async_remote_copy(
                src_ref=edge_out.at[slot, pl.ds(LINES - 16, 16)],
                dst_ref=halo.at[slot, pl.ds(LINES, 16)],
                send_sem=p_send.at[slot],
                recv_sem=p_recv.at[slot],
                device_id={"space": target, "tm": other},
                device_id_type=MESH,
            )
        )

    await_chip(chip)
    arrive(chip)
    forward([chip])

    def pair(j, carry):
        def one(i, carry):
            c = chip_at(jnp.where(i == 0, j, -j))
            await_chip(c)
            arrive(c)
            return carry

        lax.fori_loop(0, 2, one, 0)

        @pl.when(j < 3)
        def _():
            forward([chip_at(j), chip_at(-j)])

        return carry

    lax.fori_loop(1, 4, pair, 0)
    forward([chip_at(3)])
    last = chip_at(4)
    await_chip(last)
    before[0].start()
    arrive(last, grad=False)
    for slot in range(2):
        edge_out[slot] = edge[slot].astype(BF16)
    for copy in columns + before[1:]:
        copy.start()
    late_gradient(last)
    forward([chip_at(-3), last])
    before[0].wait_recv()
    second = jnp.where(tm == 0, 0.0, 1.0)
    for i in range(2):
        x = arrp[ROWS * i : ROWS * i + ROWS].astype(F32).reshape(ROWS * COLS, CIN)
        _, value, twice = activate(x, 0.5 * gain[...])
        put_hidden(hidp, i, (value * twice).astype(BF16).astype(F32) * second)
    for copy in columns + before[1:]:
        copy.wait_recv()

    for copy in sends + started + columns + before:
        copy.wait_send()


def finish(w, acc, hidp, halo, gbuf, out_hbm, gi_hbm, hrows, full, obuf, sem):
    ready = pltpu.make_async_copy(gbuf, gi_hbm, sem.at[0])
    ready.start()
    me = lax.axis_index("space")
    second = jnp.where(lax.axis_index("tm") == 0, 0.0, 1.0)
    has = (jnp.where(me > 0, 1.0, 0.0), jnp.where(me < STRIPS - 1, 1.0, 0.0))
    full[...] = acc[0:LINES]

    count = LINES + 8
    line = lax.broadcasted_iota(jnp.int32, (count, CIN), 0)
    row = lax.rem(line, ROWS)
    for slot in range(2):
        got = halo[slot].astype(F32)
        value = jnp.concatenate([got[LINES + 8 :] * second, got[0:LINES]], axis=0) * has[slot]
        hrows[slot, :, 0:CIN] = jnp.where(row == 0, 0.0, pltpu.roll(value, 1, 0))
        hrows[slot, :, CIN : 2 * CIN] = value
        hrows[slot, :, 2 * CIN :] = jnp.where(
            row == ROWS - 1, 0.0, pltpu.roll(value, count - 1, 0)
        )

    frame = ROWS * COLS
    shares = [jnp.zeros((n, COUT), F32) for n in (2 * frame, frame, LINES, LINES)]
    for t in range(3):
        sides = [hrows[slot, t * ROWS : t * ROWS + LINES].astype(BF16) for slot in range(2)]
        for h in range(3):
            for c in range(3):
                takes = []
                if t < 2:
                    lines = hidp[t:2, h : h + ROWS, :, c * CIN : (c + 1) * CIN]
                    takes.append((t, lines.reshape((2 - t) * frame, CIN)))
                if c != 1:
                    takes.append((2 + c // 2, sides[c // 2][:, h * CIN : (h + 1) * CIN]))
                if not takes:
                    continue
                product = mm(
                    takes[0][1] if len(takes) == 1 else jnp.concatenate([v for _, v in takes], 0),
                    w[3 * t + h, c * CIN : (c + 1) * CIN],
                )
                start = 0
                for share, v in takes:
                    shares[share] = shares[share] + product[start : start + v.shape[0]]
                    start += v.shape[0]

    full[0:8] += shares[0].reshape(8, COLS, COUT)
    full[0:ROWS] += shares[1].reshape(ROWS, COLS, COUT)
    for col, share in ((0, shares[2]), (COLS - 1, shares[3])):
        full[:, col, :] = full[:, col, :] + share
    obuf[...] = full[...].astype(BF16)
    result = pltpu.make_async_copy(obuf, out_hbm, sem.at[1])
    result.start()
    ready.wait()
    result.wait()


def local(latents, norm_gain, conv_weight, skip_weight, cotangent):
    hbm = pl.BlockSpec(memory_space=pl.ANY)
    dma = pltpu.SemaphoreType.DMA
    vmem = pl.BlockSpec(memory_space=pltpu.VMEM)
    parts = pl.pallas_call(
        kernel,
        out_shape=(
            pltpu.VMEM((9, 3 * CIN, COUT), BF16),
            pltpu.VMEM((LINES + 8, COLS, COUT), F32),
            pltpu.VMEM((2, ROWS + 2, COLS, 3 * CIN), BF16),
            pltpu.VMEM((2, LINES + 16, CIN), BF16),
            pltpu.VMEM((LINES, COLS, CIN), BF16),
        ),
        in_specs=[hbm] * 5,
        out_specs=(vmem,) * 5,
        scratch_shapes=[
            pltpu.VMEM((CIN, COUT), BF16),
            pltpu.VMEM((1, CIN), F32),
            pltpu.VMEM((LINES, COLS, COUT), BF16),
            pltpu.VMEM((LINES, COLS, CIN), BF16),
            pltpu.VMEM((8, COLS, CIN), BF16),
            pltpu.VMEM((8, COLS, COUT), BF16),
            pltpu.VMEM((2, LINES, COUT), BF16),
            pltpu.VMEM((2, LINES + 16, COUT), BF16),
            pltpu.VMEM((LINES + 8, 32, COUT), F32),
            pltpu.VMEM((STRIPS + 2, ROWS + 2, COLS, 3 * COUT), BF16),
            pltpu.VMEM((LINES, COLS, CIN), F32),
            pltpu.VMEM((LINES, COLS, CIN), F32),
            pltpu.VMEM((STRIPS, ROWS + 2, COLS, 3 * CIN), BF16),
            pltpu.VMEM((8, COLS, CIN), F32),
            pltpu.VMEM((2, LINES, CIN), F32),
            pltpu.VMEM((2, LINES, CIN), BF16),
            dma((3 + 9,)),
            dma,
            dma((STRIPS - 1,)),
            dma((STRIPS,)),
            dma((2, 2)),
            dma((2, 2)),
            dma,
            dma,
            dma((2,)),
            dma((2,)),
            dma((3,)),
            dma((3,)),
        ],
        compiler_params=pltpu.CompilerParams(
            collective_id=0, has_side_effects=True, vmem_limit_bytes=53 * 2**20
        ),
        cost_estimate=pl.CostEstimate(
            flops=2 * CELLS * CIN * COUT * 56, bytes_accessed=11 * 2**20, transcendentals=CELLS * CIN
        ),
    )(
        latents.reshape(ROWS, STRIPS * COLS, CIN),
        norm_gain.reshape(1, CIN),
        conv_weight.reshape(9, 3 * CIN, COUT),
        skip_weight,
        cotangent.reshape(LINES, COLS, COUT),
    )
    out, grad_input = pl.pallas_call(
        finish,
        out_shape=(
            jax.ShapeDtypeStruct((LINES, COLS, COUT), BF16),
            jax.ShapeDtypeStruct((LINES, COLS, CIN), BF16),
        ),
        in_specs=[vmem] * 5,
        out_specs=(hbm, hbm),
        scratch_shapes=[
            pltpu.VMEM((2, LINES + 8, 3 * CIN), F32),
            pltpu.VMEM((LINES, COLS, COUT), F32),
            pltpu.VMEM((LINES, COLS, COUT), BF16),
            dma((2,)),
        ],
        compiler_params=pltpu.CompilerParams(vmem_limit_bytes=16 * 2**20),
    )(*parts)
    return (
        out.reshape(STRIPS, 1, ROWS, COLS, COUT),
        grad_input.reshape(STRIPS, 1, ROWS, COLS, CIN),
    )


def solution(mesh):
    placed = (
        P(("dp", "tm", "space"), None, None, None),
        P(),
        P(),
        P(),
        P(("dp", "tm"), "space", None, None, None),
    )
    return jax.shard_map(
        local,
        mesh=mesh,
        in_specs=placed,
        out_specs=(
            P(("dp", "tm"), "space", None, None, None),
            P(("dp", "tm"), "space", None, None, None),
        ),
        check_vma=False,
    )
```
